128 devices in a mesh: row: 16 (over z, y_lo, core), col: 8 (over y_hi, x).
Axes of the slice: x: 4, y: 4 (y_hi: 2, y_lo: 2; y = y_hi * 2 + y_lo), z: 4, core: 2. Of those that a mesh axis runs over, the one named last changes fastest.
Arguments:
- latent: bfloat16 [512, 1024, 256], P('row', 'col'), may hold values from -20.2 to 20.2
- w_expand: bfloat16 [256, 1024], replicated, may hold values from -0.375 to 0.375
- w_depth: bfloat16 [3, 3, 1024], replicated, may hold values from -2 to 2
- squeeze_down: bfloat16 [1024, 64], replicated, may hold values from -0.75 to 0.75
- squeeze_up: bfloat16 [64, 1024], replicated, may hold values from -0.75 to 0.75
- w_project: bfloat16 [1024, 256], replicated, may hold values from -0.75 to 0.75
- norm_gain: float32 [2, 2, 256], replicated, may hold values from 0.1 to 1.9
- attend_in: bfloat16 [2, 256, 768], replicated, may hold values from -0.375 to 0.375
- attend_out: bfloat16 [2, 256, 256], replicated, may hold values from -0.375 to 0.375
- offset_bias: float32 [2, 8, 15, 15], replicated, may hold values from -4 to 310
- mixer_up: bfloat16 [2, 256, 1024], replicated, may hold values from -0.375 to 0.375
- mixer_down: bfloat16 [2, 1024, 256], replicated, may hold values from -0.1875 to 0.1875
Outputs:
- block_out: bfloat16 [512, 1024, 256], P('row', 'col')
The draws below stay inside these ranges and needn't reach their ends.
All inputs are finite; a program needn't handle non-finite values.
Results may differ from the reference program's by a relative error of at most 0.013.
Values may be sent and summed in bfloat16 or wider, within the bound.
A program may use at most 128 MiB of HBM per device.

```python
import math
import jax
import jax.numpy as jnp
from jax import lax

C = 256
HID = 1024
SE = 64
MLP = 1024
HEADS = 8
WIN = 8
H_DEV = 32
NH = 512
NW = 1024


def draw_latent(key, part):
    key = jax.random.fold_in(key, 11)
    key_values, key_rough = jax.random.split(key)
    row_pos = jnp.arange(NH, dtype=jnp.float32)[:, None, None] / (NH - 1)
    col_pos = jnp.arange(NW, dtype=jnp.float32)[None, :, None] / (NW - 1)
    roughness = jax.random.uniform(key_rough, (NH, NW, 1), jnp.float32, 0.6, 1.4)
    values = jnp.clip(jax.random.normal(key_values, (NH, NW, C), jnp.float32), -4.0, 4.0)
    scaling = 0.4 * jnp.exp(math.log(3.0) * (row_pos + col_pos))
    return (values * scaling * roughness).astype(jnp.bfloat16)


def draw_offset_bias(key, part):
    key = jax.random.fold_in(key, 23)
    key_base = jax.random.fold_in(key, 0)
    span_size = 2 * WIN - 1
    base_values = jnp.clip(jax.random.normal(key_base, (2, HEADS, span_size, span_size), jnp.float32), -4.0, 4.0)
    return base_values


def noise(rng, dims, scale, reach, kind=jnp.bfloat16):
    result = scale * jax.random.normal(rng, dims, jnp.float32)
    return jnp.clip(result, min=-reach, max=reach).astype(kind)


def setup_inputs(seed: int = 0) -> dict:
    seeds = jax.random.split(jax.random.key(seed), 13)
    return {
        "latent": draw_latent(jax.random.fold_in(seeds[12], 71), 0),
        "w_expand": noise(seeds[1], (C, HID), C ** -0.5, 0.375),
        "w_depth": noise(seeds[2], (3, 3, HID), 9 ** -0.5, 2.0),
        "squeeze_down": noise(seeds[3], (HID, SE), SE ** -0.5, 0.75),
        "squeeze_up": noise(seeds[4], (SE, HID), SE ** -0.5, 0.75),
        "w_project": noise(seeds[5], (HID, C), (HID // 16) ** -0.5, 0.75),
        "norm_gain": jnp.clip(1.0 + 0.18 * jax.random.normal(seeds[6], (2, 2, C), jnp.float32), 0.1, 1.9),
        "attend_in": noise(seeds[7], (2, C, 3 * C), C ** -0.5, 0.375),
        "attend_out": noise(seeds[8], (2, C, C), C ** -0.5, 0.375),
        "offset_bias": draw_offset_bias(jax.random.fold_in(seeds[12], 71), 0),
        "mixer_up": noise(seeds[10], (2, C, MLP), C ** -0.5, 0.375),
        "mixer_down": noise(seeds[11], (2, MLP, C), MLP ** -0.5, 0.1875),
    }


epsilon = 1e-05

def gelu_tanh(values):
    return jax.nn.gelu(values, approximate=True)

def rounded(values):
    return lax.optimization_barrier(values.astype(jnp.bfloat16))

def layer_norm(cell_rows, gain_row):
    floats = cell_rows.astype(jnp.float32)
    centre = floats - lax.optimization_barrier(jnp.mean(floats, axis=-1, keepdims=True))
    spread = lax.optimization_barrier(jnp.mean(centre * centre, axis=-1, keepdims=True))
    return rounded(centre * lax.rsqrt(spread + epsilon) * gain_row)

def bias_matrix(offset_table):
    cell_ids = jnp.arange(WIN * WIN)
    row_of = cell_ids // WIN
    col_of = cell_ids % WIN
    row_gap = row_of[:, None] - row_of[None, :] + WIN - 1
    col_gap = col_of[:, None] - col_of[None, :] + WIN - 1
    return offset_table[:, row_gap, col_gap]

def attend(normed, weight_in, weight_out, offset_terms):
    window_count, cell_count, feature_count = normed.shape
    head_count = offset_terms.shape[0]
    head_size = feature_count // head_count
    packed = rounded(jnp.dot(normed.reshape(-1, feature_count), weight_in, preferred_element_type=jnp.float32))
    packed = packed.reshape(window_count, cell_count, 3, head_count, head_size).astype(jnp.float32)
    scores = jnp.einsum('nqhd,nkhd->nhqk', packed[:, :, 0], packed[:, :, 1]) / math.sqrt(head_size) + offset_terms[None]
    highest = lax.optimization_barrier(jnp.max(scores, axis=-1, keepdims=True))
    raised = jnp.exp(scores - highest)
    weights = rounded(raised / lax.optimization_barrier(jnp.sum(raised, axis=-1, keepdims=True)))
    mixture = rounded(jnp.einsum('nhqk,nkhd->nqhd', weights.astype(jnp.float32), packed[:, :, 2]))
    product = jnp.dot(mixture.reshape(-1, feature_count), weight_out, preferred_element_type=jnp.float32)
    return product.reshape(window_count, cell_count, feature_count)

def window_section(cell_rows, gain_pair, weight_in, weight_out, offset_terms, weight_up, weight_down):
    feature_count = cell_rows.shape[-1]
    attended = rounded(cell_rows.astype(jnp.float32) + attend(layer_norm(cell_rows, gain_pair[0]), weight_in, weight_out, offset_terms))
    normed = layer_norm(attended, gain_pair[1]).reshape(-1, feature_count)
    raised = rounded(gelu_tanh(jnp.dot(normed, weight_up, preferred_element_type=jnp.float32)))
    lowered = jnp.dot(raised, weight_down, preferred_element_type=jnp.float32).reshape(cell_rows.shape)
    return rounded(attended.astype(jnp.float32) + lowered)

def reference(latent, w_expand, w_depth, squeeze_down, squeeze_up, w_project, norm_gain, attend_in, attend_out, offset_bias, mixer_up, mixer_down):
    padded = jnp.pad(latent, ((1, 1), (1, 1), (0, 0)))
    starts = jnp.arange(NH // H_DEV, dtype=jnp.int32) * H_DEV
    tap_weights = w_depth.astype(jnp.float32)

    def activated(first_row):
        slab_rows = lax.dynamic_slice_in_dim(padded, first_row, H_DEV + 2, 0)
        hidden = rounded(gelu_tanh(jnp.dot(slab_rows.reshape(-1, C), w_expand, preferred_element_type=jnp.float32)))
        hidden = hidden.reshape(H_DEV + 2, NW + 2, HID)
        depthwise = jnp.zeros((H_DEV, NW, HID), jnp.float32)
        for shift_row in range(3):
            for shift_col in range(3):
                depthwise = depthwise + tap_weights[shift_row, shift_col] * hidden[shift_row:shift_row + H_DEV, shift_col:shift_col + NW].astype(jnp.float32)
        return gelu_tanh(depthwise)
    column_sums = lax.map(lambda first_row: lax.optimization_barrier(jnp.sum(activated(first_row), axis=(0, 1))), starts)
    squeeze = lax.optimization_barrier(jnp.sum(column_sums, axis=0)) / (NH * NW)
    hidden_gate = jax.nn.silu(jnp.dot(squeeze[None, :], squeeze_down.astype(jnp.float32), precision=lax.Precision.HIGHEST))
    excite = jax.nn.sigmoid(jnp.dot(hidden_gate, squeeze_up.astype(jnp.float32), precision=lax.Precision.HIGHEST))[0]

    def projected(first_row):
        gated_act = rounded(activated(first_row) * excite)
        branch = jnp.dot(gated_act.reshape(-1, HID), w_project, preferred_element_type=jnp.float32)
        shortcut = lax.dynamic_slice_in_dim(latent, first_row, H_DEV, 0).reshape(-1, C).astype(jnp.float32)
        return rounded(shortcut + branch).reshape(H_DEV, NW, C)
    conv_out = lax.map(projected, starts).reshape(NH, NW, C)
    block_terms = bias_matrix(offset_bias[0])
    grid_terms = bias_matrix(offset_bias[1])

    def block_band(one_band):
        window_rows = one_band.transpose(1, 0, 2, 3).reshape(NW // WIN, WIN * WIN, C)
        finished = window_section(window_rows, norm_gain[0], attend_in[0], attend_out[0], block_terms, mixer_up[0], mixer_down[0])
        return finished.reshape(NW // WIN, WIN, WIN, C).transpose(1, 0, 2, 3)
    row_bands = conv_out.reshape(NH // WIN, WIN, NW // WIN, WIN, C)
    blocked = lax.map(block_band, row_bands).reshape(NH, NW, C)
    stride_row = NH // WIN
    stride_col = NW // WIN
    spread = blocked.reshape(WIN, stride_row, WIN, stride_col, C).transpose(1, 3, 0, 2, 4)

    def grid_band(one_band):
        window_rows = one_band.reshape(stride_col, WIN * WIN, C)
        finished = window_section(window_rows, norm_gain[1], attend_in[1], attend_out[1], grid_terms, mixer_up[1], mixer_down[1])
        return finished.reshape(stride_col, WIN, WIN, C)
    gathered = lax.map(grid_band, spread)
    return gathered.transpose(2, 0, 3, 1, 4).reshape(NH, NW, C)
```

```python
import functools
import math

import jax
import jax.numpy as jnp
from jax import lax
from jax.experimental import pallas as pl
from jax.experimental.pallas import tpu as pltpu
from jax.sharding import PartitionSpec as P

MESH = pl.DeviceIdType.MESH
BF = jnp.bfloat16
F32 = jnp.float32
WIN = 8
CELLS = 64
EPSILON = 1e-05
LOG2E = 1.4426950408889634
ROWS, COLS = 16, 8
BANDS = 4
NT = (((1,), (1,)), ((), ()))


def dot(a, b):
    return jnp.dot(a, b, preferred_element_type=F32)


def dot_nt(a, b):
    return lax.dot_general(a, b, NT, preferred_element_type=F32)


def twice_gelu(v):
    c1 = jnp.asarray(0.7978845608, v.dtype)
    c2 = jnp.asarray(0.7978845608 * 0.044715, v.dtype)
    return v + v * jnp.tanh(v * (c1 + c2 * (v * v)))


def normalise(x, gain):
    mean = jnp.sum(x, axis=-1, keepdims=True) * (1.0 / 256)
    centre = x - mean
    var = jnp.sum(centre * centre, axis=-1, keepdims=True) * (1.0 / 256)
    return (centre * lax.rsqrt(var + EPSILON) * gain).astype(BF)


def put(ref, rows, value):
    ref[0, rows, :] = value[:, :128]
    ref[1, rows, :] = value[:, 128:]


def take(ref, start, count, stride):
    rows = pl.ds(start, count, stride=stride)
    return jnp.concatenate([ref[0, rows, :], ref[1, rows, :]], axis=1)


def front_kernel(
    latent, w_expand, taps, down, up_t, w_project,
    act_out, w_out,
    flat, lat, edge_l, edge_r, halo_l, halo_r, halo_t, halo_b, corners, hid, hid_edge, act,
    total, ar1, ar2, send_sems, recv_sems, ar_send, ar_recv, out_sems,
):
    row, col = lax.axis_index("row"), lax.axis_index("col")
    up, dn = lax.rem(row + ROWS - 1, ROWS), lax.rem(row + 1, ROWS)
    lf, rt = lax.rem(col + COLS - 1, COLS), lax.rem(col + 1, COLS)
    barrier = pltpu.get_barrier_semaphore()
    neighbours = ((row, lf), (row, rt), (up, col), (dn, col), (up, lf), (up, rt), (dn, lf), (dn, rt))
    for who in neighbours:
        pl.semaphore_signal(barrier, inc=1, device_id=who, device_id_type=MESH)

    def greet_row(o, c):
        pl.semaphore_signal(barrier, inc=1, device_id=(lax.rem(row + o, ROWS), col), device_id_type=MESH)
        return c

    def greet_col(o, c):
        pl.semaphore_signal(barrier, inc=1, device_id=(row, lax.rem(col + o, COLS)), device_id_type=MESH)
        return c

    lax.fori_loop(1, ROWS, greet_row, 0)
    lax.fori_loop(1, COLS, greet_col, 0)

    def spread(y, c):
        put(flat, pl.ds(pl.multiple_of(y * 128, 128), 128), latent[y].astype(F32))
        for v in range(8):
            lat[y, v] = take(flat, y * 128 + v, 16, 8).astype(BF)
        return c

    lax.fori_loop(0, 32, spread, 0)
    edge_l[...] = take(flat, 0, 32, 128).astype(BF)
    edge_r[...] = take(flat, 127, 32, 128).astype(BF)
    pl.semaphore_wait(barrier, 8 + ROWS - 1 + COLS - 1)
    first, last = pl.ds(0, 16), pl.ds(16, 16)
    moves = (
        (edge_l, halo_r, (row, lf)),
        (edge_r, halo_l, (row, rt)),
        (lat.at[0], halo_b, (up, col)),
        (lat.at[31], halo_t, (dn, col)),
        (edge_l.at[first], corners.at[3], (up, lf)),
        (edge_r.at[first], corners.at[2], (up, rt)),
        (edge_l.at[last], corners.at[1], (dn, lf)),
        (edge_r.at[last], corners.at[0], (dn, rt)),
    )
    copies = []
    for i, (src, dst, who) in enumerate(moves):
        copy = pltpu.make_async_remote_copy(
            src_ref=src, dst_ref=dst, send_sem=send_sems.at[i], recv_sem=recv_sems.at[i], device_id=who, device_id_type=MESH
        )
        copy.start()
        copies.append(copy)

    def expand(i, c):
        cells = lat[pl.ds(i * 4, 4)].reshape(512, 256)
        for t in range(4):
            part = pl.ds(t * 256, 256)
            h = twice_gelu(dot(cells, w_expand[:, part]).astype(BF))
            hid[pl.ds(1 + i * 4, 4), 1:9, :, part] = h.reshape(4, 8, 16, 256)
        return c

    lax.fori_loop(0, 8, expand, 0)
    for copy in copies:
        copy.wait()
    zero = jnp.zeros((), BF)
    top = jnp.where(row > 0, halo_t[...], zero).reshape(128, 256)
    bottom = jnp.where(row < ROWS - 1, halo_b[...], zero).reshape(128, 256)
    rows2 = jnp.concatenate([top, bottom], axis=0)
    left = jnp.concatenate([
        halo_l[...], jnp.where(row > 0, corners[0], zero), jnp.where(row < ROWS - 1, corners[2], zero)], axis=0)
    right = jnp.concatenate([
        halo_r[...], jnp.where(row > 0, corners[1], zero), jnp.where(row < ROWS - 1, corners[3], zero)], axis=0)
    left = jnp.where(col > 0, left, zero)
    right = jnp.where(col < COLS - 1, right, zero)
    sides = jnp.concatenate([left, right], axis=0)
    for t in range(4):
        part = pl.ds(t * 256, 256)
        h = twice_gelu(dot(rows2, w_expand[:, part]).astype(BF)).reshape(2, 8, 16, 256)
        hid[0, 1:9, :, part] = h[0]
        hid[33, 1:9, :, part] = h[1]
        hid_edge[:, part] = twice_gelu(dot(sides, w_expand[:, part]).astype(BF)).astype(F32)

    lane_n = lax.broadcasted_iota(jnp.int32, (16, 1024), 0)

    def wrap(y, c):
        place = jnp.where(y == 0, 47, jnp.where(y == 33, 48, y - 1))
        before = pltpu.roll(hid[y, 8].astype(F32), 1, 0)
        hid[y, 0] = jnp.where(lane_n == 0, hid_edge[pl.ds(place, 1), :], before).astype(BF)
        after = pltpu.roll(hid[y, 1].astype(F32), 15, 0)
        hid[y, 9] = jnp.where(lane_n == 15, hid_edge[pl.ds(place + 64, 1), :], after).astype(BF)
        return c

    lax.fori_loop(0, 34, wrap, 0)

    for t in range(8):
        part = pl.ds(t * 128, 128)
        weights = [taps[i, :, part] for i in range(9)]

        def depthwise(y, sums):
            acc = None
            for r in range(3):
                cells = hid[y + r, :, :, part]
                for s in range(3):
                    term = weights[r * 3 + s][None] * cells[s : s + 8]
                    acc = term if acc is None else acc + term
            a = twice_gelu(acc)
            act[y, :, :, part] = a
            b = a[:4] + a[4:]
            b = b[:2] + b[2:]
            return sums + (b[0] + b[1]).astype(F32)

        sums = lax.fori_loop(0, 32, depthwise, jnp.zeros((16, 128), F32))
        total[t : t + 1, :] = jnp.sum(sums, axis=0, keepdims=True)
        pltpu.make_async_copy(act.at[:, :, :, part], act_out.at[:, :, :, part], out_sems.at[t]).start()

    ar1[row] = total[...]

    def send_row(o, c):
        pltpu.make_async_remote_copy(
            src_ref=total, dst_ref=ar1.at[row], send_sem=ar_send.at[0], recv_sem=ar_recv.at[0],
            device_id=(lax.rem(row + o, ROWS), col), device_id_type=MESH).start()
        return c

    lax.fori_loop(1, ROWS, send_row, 0)
    rest = ar1.at[pl.ds(0, ROWS - 1)]
    pltpu.make_async_copy(rest, rest, ar_recv.at[0]).wait()
    pltpu.make_async_copy(rest, rest, ar_send.at[0]).wait()
    ar2[col] = jnp.sum(ar1[...], axis=0)

    def send_col(o, c):
        pltpu.make_async_remote_copy(
            src_ref=ar2.at[col], dst_ref=ar2.at[col], send_sem=ar_send.at[1], recv_sem=ar_recv.at[1],
            device_id=(row, lax.rem(col + o, COLS)), device_id_type=MESH).start()
        return c

    lax.fori_loop(1, COLS, send_col, 0)
    rest = ar2.at[pl.ds(0, COLS - 1)]
    pltpu.make_async_copy(rest, rest, ar_recv.at[1]).wait()
    pltpu.make_async_copy(rest, rest, ar_send.at[1]).wait()
    total[...] = jnp.sum(ar2[...], axis=0) * (0.5 / (512 * 1024))
    squeeze = jnp.concatenate([total[i : i + 1, :] for i in range(8)], axis=1)
    squeeze = jnp.broadcast_to(squeeze, (8, 1024))
    gate = jnp.dot(squeeze, down[...].astype(F32), precision=lax.Precision.HIGHEST, preferred_element_type=F32)
    gate = gate * jax.nn.sigmoid(gate)
    excite = jax.nn.sigmoid(jnp.sum(up_t[...].astype(F32) * gate[0:1, :], axis=1, keepdims=True))
    w_out[...] = (w_project[...].astype(F32) * (0.5 * excite)).astype(BF)
    for t in range(8):
        part = pl.ds(t * 128, 128)
        pltpu.make_async_copy(act.at[:, :, :, part], act_out.at[:, :, :, part], out_sems.at[t]).wait()


def front(latent, w_expand, taps, down, up_t, w_project):
    vmem = pl.BlockSpec(memory_space=pltpu.VMEM)
    return pl.pallas_call(
        front_kernel,
        out_shape=(jax.ShapeDtypeStruct((32, 8, 16, 1024), BF), jax.ShapeDtypeStruct((1024, 256), BF)),
        in_specs=[vmem] * 6,
        out_specs=(pl.BlockSpec(memory_space=pl.ANY), vmem),
        scratch_shapes=[
            pltpu.VMEM((2, 4096, 128), F32),
            pltpu.VMEM((32, 8, 16, 256), BF),
            pltpu.VMEM((32, 256), BF),
            pltpu.VMEM((32, 256), BF),
            pltpu.VMEM((32, 256), BF),
            pltpu.VMEM((32, 256), BF),
            pltpu.VMEM((8, 16, 256), BF),
            pltpu.VMEM((8, 16, 256), BF),
            pltpu.VMEM((4, 16, 256), BF),
            pltpu.VMEM((34, 10, 16, 1024), BF),
            pltpu.VMEM((128, 1024), F32),
            pltpu.VMEM((32, 8, 16, 1024), BF),
            pltpu.VMEM((8, 128), F32),
            pltpu.VMEM((ROWS, 8, 128), F32),
            pltpu.VMEM((COLS, 8, 128), F32),
            pltpu.SemaphoreType.DMA((8,)),
            pltpu.SemaphoreType.DMA((8,)),
            pltpu.SemaphoreType.DMA((2,)),
            pltpu.SemaphoreType.DMA((2,)),
            pltpu.SemaphoreType.DMA((8,)),
        ],
        compiler_params=pltpu.CompilerParams(collective_id=0, has_side_effects=True, vmem_limit_bytes=56 << 20),
        name="front",
    )(latent, w_expand, taps, down, up_t, w_project)


def attention_pair(q2, k2, vt2, bias, s):
    lane = lax.broadcasted_iota(jnp.int32, (64, 256), 1)
    lane_head = lax.rem(lane, 128) // 32
    lane_win = lax.broadcasted_iota(jnp.int32, (64, 128), 1) // 64
    zero = jnp.zeros((), BF)
    z = jnp.zeros((64, 128), BF)
    z32 = jnp.zeros((32, 128), BF)
    scale = LOG2E / math.sqrt(32)
    out = []
    for half in range(2):
        f = slice(half * 128, half * 128 + 128)
        qh, kh, vh = q2[:, f], k2[:, f], vt2[f, :]
        q_block = jnp.concatenate(
            [jnp.concatenate([qh[:64], z], axis=1), jnp.concatenate([z, qh[64:]], axis=1)], axis=0)
        k_both = jnp.concatenate([kh[:64], kh[64:]], axis=1)
        k_block = jnp.concatenate([jnp.where(lane_head == h, k_both, zero) for h in range(4)], axis=0)
        scores = dot_nt(k_block, q_block) * scale + bias[s, half]
        scores = scores.reshape(4, 64, 128)
        raised = jnp.exp2(scores - jnp.max(scores, axis=1, keepdims=True))
        inverse = 1.0 / jnp.sum(raised, axis=1, keepdims=True)
        weights = raised.astype(BF)
        rhs = jnp.concatenate(
            [jnp.where(lane_win == w, weights[h], zero) for h in range(4) for w in range(2)], axis=0)
        lhs = jnp.concatenate(
            [jnp.concatenate([vh[h * 32 : h * 32 + 32] if g == h else z32 for g in range(4)], axis=1) for h in range(4)],
            axis=0)
        mixed = dot(lhs, rhs).reshape(4, 32, 128) * inverse
        out.append(mixed.reshape(128, 128))
    return jnp.concatenate(out, axis=0)


def section_chunk(x, s, gains, w_qk, w_vt, w_o, w_up, w_down, bias):
    normed = normalise(x, gains[s, 0:1])
    qk = dot(normed, w_qk[s]).astype(BF)
    vt = dot_nt(w_vt[s], normed).astype(BF)
    mixes = []
    for p in range(2):
        r = slice(p * 128, p * 128 + 128)
        mixed = attention_pair(qk[r, :256], qk[r, 256:], vt[:, r], bias, s)
        mixes.append(mixed.T.astype(BF))
    mix = jnp.concatenate(mixes, axis=0)
    attended = (x + dot(mix, w_o[s])).astype(BF).astype(F32)
    normed = normalise(attended, gains[s, 1:2])
    lowered = jnp.zeros((256, 256), F32)
    for t in range(4):
        part = slice(t * 256, t * 256 + 256)
        up = twice_gelu(dot(normed, w_up[s, :, part]).astype(BF))
        lowered = lowered + dot(up, w_down[s, part, :])
    return attended + lowered


def sections_kernel(
    act, latent, w_project, gains, w_qk, w_vt, w_o, w_up, w_down, bias,
    returned,
    act_buf, conv, res, fwd_send, fwd_recv, back_send,
    act_sems, fs_sems, fr_sems, bs_sems, br_sems,
):
    row, col = lax.axis_index("row"), lax.axis_index("col")
    core, g = lax.rem(row, 2), row // 2
    me = g * 8 + col
    z, ylo, yhi, x = g // 2, lax.rem(g, 2), col // 4, lax.rem(col, 4)
    y = yhi * 2 + ylo
    barrier = pltpu.get_barrier_semaphore()

    def partner(o):
        dz = lax.rem(o, 4)
        x2 = lax.rem(x + o // 4 + dz, 4)
        y2 = lax.rem(y + o // 16 + dz, 4)
        z2 = lax.rem(z + dz, 4)
        g2, col2 = z2 * 2 + lax.rem(y2, 2), (y2 // 2) * 4 + x2
        return g2 * 8 + col2, (g2 * 2 + core, col2)

    def greet(o, c):
        _, who = partner(o)
        pl.semaphore_signal(barrier, inc=1, device_id=who, device_id_type=MESH)
        return c

    lax.fori_loop(1, 64, greet, 0)

    def fetch(k):
        slot = lax.rem(k, 2)
        return pltpu.make_async_copy(act.at[pl.ds(k * 8, 8)], act_buf.at[slot], act_sems.at[slot])

    def run_chunks(s, sink):
        def chunk(i, c):
            rows = pl.ds(pl.multiple_of(i * 256, 256), 256)
            sink(i, rows, section_chunk(res[rows, :], s, gains, w_qk, w_vt, w_o, w_up, w_down, bias))
            return c

        lax.fori_loop(0, 4, chunk, 0)

    fetch(0).start()
    pl.semaphore_wait(barrier, 63)

    def forward(k, c):
        @pl.when(k < BANDS - 1)
        def _():
            fetch(k + 1).start()

        fetch(k).wait()
        slot = lax.rem(k, 2)

        def project(i, c2):
            cells = act_buf[slot, pl.ds(i * 2, 2)].reshape(256, 1024)
            put(conv, pl.ds(pl.multiple_of(i * 256, 256), 256), dot(cells, w_project[...]))
            return c2

        lax.fori_loop(0, 4, project, 0)

        def regroup(n, c2):
            branch = take(conv, n, 64, 16)
            short = latent[pl.ds(k * 8, 8), pl.ds(pl.multiple_of(n // 2 * 16, 16), 16), :].astype(F32)
            short = jnp.where(lax.rem(n, 2) == 0, short[:, :8], short[:, 8:]).reshape(64, 256)
            res[pl.ds(pl.multiple_of(n * 64, 64), 64), :] = (branch + short).astype(BF).astype(F32)
            return c2

        lax.fori_loop(0, 16, regroup, 0)

        def sink(i, rows, value):
            fwd_send[k, pl.ds(i * 16, 16)] = value.astype(BF).reshape(16, 16, 256)

        run_chunks(0, sink)
        pltpu.make_async_copy(fwd_send.at[k, me], fwd_recv.at[k, me], fr_sems.at[k]).start()

        def send(o, c2):
            t, who = partner(o)
            pltpu.make_async_remote_copy(
                src_ref=fwd_send.at[k, t], dst_ref=fwd_recv.at[k, me], send_sem=fs_sems.at[k], recv_sem=fr_sems.at[k],
                device_id=who, device_id_type=MESH).start()
            return c2

        lax.fori_loop(1, 64, send, 0)
        return c

    lax.fori_loop(0, BANDS, forward, 0)

    def backward(k, c):
        pltpu.make_async_copy(fwd_recv.at[k], fwd_recv.at[k], fr_sems.at[k]).wait()

        def unpack(i, c2):
            put(conv, pl.ds(pl.multiple_of(i * 256, 256), 256), fwd_recv[k, pl.ds(i * 16, 16)].reshape(256, 256).astype(F32))
            return c2

        lax.fori_loop(0, 4, unpack, 0)

        def regroup(n, c2):
            res[pl.ds(pl.multiple_of(n * 64, 64), 64), :] = take(conv, n, 64, 16)
            return c2

        lax.fori_loop(0, 16, regroup, 0)

        def sink(i, rows, value):
            put(conv, rows, value)

        run_chunks(1, sink)

        def repack(t, c2):
            back_send[k, t] = take(conv, t, 16, 64).astype(BF)
            return c2

        lax.fori_loop(0, 64, repack, 0)
        pltpu.make_async_copy(back_send.at[k, me], returned.at[k, me], br_sems.at[k]).start()

        def send(o, c2):
            t, who = partner(o)
            pltpu.make_async_remote_copy(
                src_ref=back_send.at[k, t], dst_ref=returned.at[k, me], send_sem=bs_sems.at[k], recv_sem=br_sems.at[k],
                device_id=who, device_id_type=MESH).start()
            return c2

        lax.fori_loop(1, 64, send, 0)
        return c

    lax.fori_loop(0, BANDS, backward, 0)

    def finish(k, c):
        pltpu.make_async_copy(returned.at[k], returned.at[k], br_sems.at[k]).wait()
        for sems, buf in ((fs_sems, fwd_send), (bs_sems, back_send)):
            sent = buf.at[k, pl.ds(0, 63)]
            pltpu.make_async_copy(sent, sent, sems.at[k]).wait()
        return c

    lax.fori_loop(0, BANDS, finish, 0)


def sections(act, latent, w_project, gains, w_qk, w_vt, w_o, w_up, w_down, bias):
    vmem = pl.BlockSpec(memory_space=pltpu.VMEM)
    block = (BANDS, 64, 16, 256)
    return pl.pallas_call(
        sections_kernel,
        out_shape=jax.ShapeDtypeStruct(block, BF),
        in_specs=[pl.BlockSpec(memory_space=pl.ANY)] + [vmem] * 9,
        out_specs=pl.BlockSpec(memory_space=pl.ANY),
        scratch_shapes=[
            pltpu.VMEM((2, 8, 8, 16, 1024), BF),
            pltpu.VMEM((2, 1024, 128), F32),
            pltpu.VMEM((1024, 256), F32),
            pltpu.VMEM(block, BF),
            pltpu.VMEM(block, BF),
            pltpu.VMEM(block, BF),
            pltpu.SemaphoreType.DMA((2,)),
            pltpu.SemaphoreType.DMA((BANDS,)),
            pltpu.SemaphoreType.DMA((BANDS,)),
            pltpu.SemaphoreType.DMA((BANDS,)),
            pltpu.SemaphoreType.DMA((BANDS,)),
        ],
        compiler_params=pltpu.CompilerParams(collective_id=1, has_side_effects=True, vmem_limit_bytes=56 << 20),
        name="sections",
    )(act, latent, w_project, gains, w_qk, w_vt, w_o, w_up, w_down, bias)


def bias_tables(offset_bias):
    ids = jnp.arange(CELLS)
    r, c = ids // WIN, ids % WIN
    index = (r[None, :] - r[:, None] + 7) * 15 + c[None, :] - c[:, None] + 7
    selector = (jnp.arange(225)[:, None] == index.reshape(1, -1)).astype(F32)
    table = jnp.dot(offset_bias.reshape(16, 225) * LOG2E, selector, precision=lax.Precision.HIGHEST)
    table = table.reshape(2, 2, 256, 64)
    return jnp.concatenate([table, table], axis=-1)


def per_device(
    latent, w_expand, w_depth, squeeze_down, squeeze_up, w_project,
    norm_gain, attend_in, attend_out, offset_bias, mixer_up, mixer_down,
):
    taps = jnp.broadcast_to((w_depth * 0.5).reshape(9, 1, 1024), (9, 16, 1024))
    act, gated_project = front(latent, w_expand, taps, squeeze_down, squeeze_up.T, w_project)
    returned = sections(
        act, latent, gated_project, norm_gain,
        attend_in[:, :, :512], attend_in[:, :, 512:].transpose(0, 2, 1), attend_out, mixer_up, mixer_down * 0.5,
        bias_tables(offset_bias),
    )
    tiles = returned.reshape(BANDS, 16, WIN, WIN, 256).transpose(0, 2, 1, 3, 4)
    return tiles.reshape(32, 128, 256)


def solution(mesh):
    in_specs = (P("row", "col", None),) + (P(),) * 11
    return jax.shard_map(
        per_device, mesh=mesh, in_specs=in_specs, out_specs=P("row", "col", None), check_vma=False
    )
```

```python
import math

import jax
import jax.numpy as jnp
from jax import lax
from jax.experimental import pallas as pl
from jax.experimental.pallas import tpu as pltpu
from jax.sharding import PartitionSpec as P

MESH = pl.DeviceIdType.MESH
BF = jnp.bfloat16
F32 = jnp.float32
EPSILON = 1e-05
LOG2E = 1.4426950408889634
ROWS, COLS = 16, 8
BANDS = 4
NT = (((1,), (1,)), ((), ()))


def dot(a, b):
    return jnp.dot(a, b, preferred_element_type=F32)


def dot_nt(a, b):
    return lax.dot_general(a, b, NT, preferred_element_type=F32)


def twice_gelu(v):
    c1 = jnp.asarray(0.7978845608, v.dtype)
    c2 = jnp.asarray(0.7978845608 * 0.044715, v.dtype)
    return v + v * jnp.tanh(v * (c1 + c2 * (v * v)))


def normalise(x, gain):
    mean = jnp.sum(x, axis=-1, keepdims=True) * (1.0 / 256)
    centre = x - mean
    var = jnp.sum(centre * centre, axis=-1, keepdims=True) * (1.0 / 256)
    return (centre * lax.rsqrt(var + EPSILON) * gain).astype(BF)


def put(ref, rows, value):
    ref[0, rows, :] = value[:, :128]
    ref[1, rows, :] = value[:, 128:]


def take(ref, start, count, stride):
    rows = pl.ds(start, count, stride=stride)
    return jnp.concatenate([ref[0, rows, :], ref[1, rows, :]], axis=1)


def lanes(value, t):
    return value[:, t * 128 : t * 128 + 128]


def attention_pair(q2, k2, vt2, bias, s):
    lane = lax.broadcasted_iota(jnp.int32, (64, 256), 1)
    lane_head = lax.rem(lane, 128) // 32
    first = lax.broadcasted_iota(jnp.int32, (32, 128), 1) < 64
    first_out = lax.broadcasted_iota(jnp.int32, (128, 128), 1) < 64
    zero = jnp.zeros((), BF)
    z = jnp.zeros((64, 128), BF)
    z32 = jnp.zeros((32, 128), BF)
    scale = LOG2E / math.sqrt(32)
    out = []
    for half in range(2):
        f = slice(half * 128, half * 128 + 128)
        qh, kh, vh = q2[:, f], k2[:, f], vt2[f, :]
        q_block = jnp.concatenate(
            [jnp.concatenate([qh[:64], z], axis=1), jnp.concatenate([z, qh[64:]], axis=1)], axis=0)
        k_both = jnp.concatenate([kh[:64], kh[64:]], axis=1)
        k_block = jnp.concatenate([jnp.where(lane_head == h, k_both, zero) for h in range(4)], axis=0)
        scores = dot_nt(k_block, q_block) * scale + bias[s, half]
        scores = scores.reshape(4, 64, 128)
        raised = jnp.exp2(scores - jnp.max(scores, axis=1, keepdims=True))
        inverse = 1.0 / jnp.sum(raised, axis=1, keepdims=True)
        weights = raised.astype(BF).reshape(256, 128)
        swapped = jnp.concatenate([vh[:, 64:], vh[:, :64]], axis=1)
        lhs = []
        for w in range(2):
            for h in range(4):
                source = (vh if h % 2 == w else swapped)[h * 32 : h * 32 + 32]
                kept = jnp.where(first, source, zero) if h % 2 == 0 else jnp.where(first, zero, source)
                lhs.append(jnp.concatenate([kept, z32] if h < 2 else [z32, kept], axis=1))
        mixed = dot(jnp.concatenate(lhs, axis=0), weights)
        mixed = jnp.where(first_out, mixed[:128], mixed[128:]).reshape(4, 32, 128) * inverse
        out.append(mixed.reshape(128, 128))
    return jnp.concatenate(out, axis=0)


def section_rows(x, s, gains, w_in, w_vt, w_o, w_up, w_down, bias):
    n = x.shape[0]
    normed = normalise(x, gains[s, 0:1])
    qk = dot(normed, w_in[s, :, :512]).astype(BF)
    vt = dot_nt(w_vt[s], normed).astype(BF)
    mixes = []
    for p in range(n // 128):
        r = slice(p * 128, p * 128 + 128)
        mixed = attention_pair(qk[r, :256], qk[r, 256:], vt[:, r], bias, s)
        mixes.append(mixed.T.astype(BF))
    mix = jnp.concatenate(mixes, axis=0)
    attended = (x + dot(mix, w_o[s])).astype(BF).astype(F32)
    normed = normalise(attended, gains[s, 1:2])
    up = [twice_gelu(dot(normed, w_up[s, :, t * 256 : t * 256 + 256]).astype(BF)) for t in range(4)]
    return attended + 0.5 * dot(jnp.concatenate(up, axis=1), w_down[s])


def bias_tables(offsets, flat, bias):
    pad = jnp.zeros((8, 113), F32)
    parts = []
    for s in range(2):
        for tile in range(2):
            acc = jnp.zeros((8, 128), F32)
            for r in range(tile * 8, min(tile * 8 + 8, 15)):
                row = jnp.concatenate([offsets[s, r] * LOG2E, pad], axis=1)
                shift = (r - tile * 8) * 16
                acc = acc + (pltpu.roll(row, shift, 1) if shift else row)
            parts.append(acc)
    table = jnp.concatenate(
        [jnp.concatenate(parts[:2], axis=1), jnp.concatenate(parts[2:], axis=1)], axis=0)
    high = table.astype(BF)
    rest = table - high.astype(F32)
    middle = rest.astype(BF)
    low = (rest - middle.astype(F32)).astype(BF)
    source = lax.broadcasted_iota(jnp.int32, (256, 128), 0)
    target = lax.broadcasted_iota(jnp.int32, (256, 128), 1)
    same_row = source // 16 == target // 8
    for key_col in range(8):
        pick = same_row & (lax.rem(source, 16) == lax.rem(target, 8) + (7 - key_col))
        pick = jnp.where(pick, 1.0, 0.0).astype(BF)
        flat[0, key_col * 16 : key_col * 16 + 16, :] = dot(high, pick) + dot(middle, pick) + dot(low, pick)
    left = lax.broadcasted_iota(jnp.int32, (8, 128), 1) < 64
    for s in range(2):
        for h in range(8):
            block = flat[0, pl.ds(s * 8 + h, 8, stride=16), :]
            for key_row in range(8):
                first = pltpu.roll(block, (128 - (7 - key_row) * 8) % 128, 1) if key_row < 7 else block
                both = jnp.where(left, first, pltpu.roll(first, 64, 1))
                start = (h % 4) * 64 + key_row * 8
                bias[s, h // 4, start : start + 8, :] = both


def kernel(
    latent_hbm, w_expand, taps, down_t, up, w_project, gains, w_in_hbm, w_o_hbm, offsets, w_up_hbm, w_down_hbm,
    out,
    latent, w_in, w_o, w_up, w_down, w_vt, bias, gated,
    flat, lat, edge_l, edge_r, halo_l, halo_r, halo_t, halo_b, corners, hid, hid_edge, act,
    total, ar1, ar2, conv, fwd_send, fwd_recv, back_send,
    load_sems, send_sems, recv_sems, ar_send, ar_recv, fs_sems, fr_sems, bs_sems, br_sems,
):
    row, col = lax.axis_index("row"), lax.axis_index("col")
    core, g = lax.rem(row, 2), row // 2
    me = g * 8 + col
    up_row, dn_row = lax.rem(row + ROWS - 1, ROWS), lax.rem(row + 1, ROWS)
    lf, rt = lax.rem(col + COLS - 1, COLS), lax.rem(col + 1, COLS)
    z, ylo, yhi, x = g // 2, lax.rem(g, 2), col // 4, lax.rem(col, 4)
    y = yhi * 2 + ylo

    def partner(o):
        dz = lax.rem(o, 4)
        x2 = lax.rem(x + o // 4 + dz, 4)
        y2 = lax.rem(y + o // 16 + dz, 4)
        z2 = lax.rem(z + dz, 4)
        g2, col2 = z2 * 2 + lax.rem(y2, 2), (y2 // 2) * 4 + x2
        return g2 * 8 + col2, (g2 * 2 + core, col2)

    loads = [
        pltpu.make_async_copy(src, dst, load_sems.at[i])
        for i, (src, dst) in enumerate(
            ((latent_hbm, latent), (w_in_hbm, w_in), (w_o_hbm, w_o), (w_up_hbm, w_up), (w_down_hbm, w_down)))
    ]
    for load in loads:
        load.start()

    barrier = pltpu.get_barrier_semaphore()
    for who in ((row, lf), (row, rt), (up_row, col), (dn_row, col), (up_row, lf), (up_row, rt), (dn_row, lf), (dn_row, rt)):
        pl.semaphore_signal(barrier, inc=1, device_id=who, device_id_type=MESH)

    def greet_row(o, c):
        pl.semaphore_signal(barrier, inc=1, device_id=(lax.rem(row + o, ROWS), col), device_id_type=MESH)
        return c

    def greet_col(o, c):
        pl.semaphore_signal(barrier, inc=1, device_id=(row, lax.rem(col + o, COLS)), device_id_type=MESH)
        return c

    def greet_partner(o, c):
        t = lax.rem(me + o, 64)
        pl.semaphore_signal(barrier, inc=1, device_id=((t // 8) * 2 + core, lax.rem(t, 8)), device_id_type=MESH)
        return c

    lax.fori_loop(1, ROWS, greet_row, 0)
    lax.fori_loop(1, COLS, greet_col, 0)
    lax.fori_loop(1, 64, greet_partner, 0)
    loads[0].wait()

    def spread(y, c):
        put(flat, pl.ds(pl.multiple_of(y * 128, 128), 128), latent[y].astype(F32))
        for v in range(8):
            for j in range(2):
                lat[j, y, v] = flat[j, pl.ds(y * 128 + v, 16, stride=8), :].astype(BF)
        return c

    lax.fori_loop(0, 32, spread, 0)
    edge_l[...] = take(flat, 0, 32, 128).astype(BF)
    edge_r[...] = take(flat, 127, 32, 128).astype(BF)
    pl.semaphore_wait(barrier, 8 + ROWS - 1 + COLS - 1 + 63)
    first, last = pl.ds(0, 16), pl.ds(16, 16)
    moves = (
        (edge_l, halo_r, (row, lf)),
        (edge_r, halo_l, (row, rt)),
        (lat.at[:, 0], halo_b, (up_row, col)),
        (lat.at[:, 31], halo_t, (dn_row, col)),
        (edge_l.at[first], corners.at[3], (up_row, lf)),
        (edge_r.at[first], corners.at[2], (up_row, rt)),
        (edge_l.at[last], corners.at[1], (dn_row, lf)),
        (edge_r.at[last], corners.at[0], (dn_row, rt)),
    )
    copies = []
    for i, (src, dst, who) in enumerate(moves):
        copy = pltpu.make_async_remote_copy(
            src_ref=src, dst_ref=dst, send_sem=send_sems.at[i], recv_sem=recv_sems.at[i], device_id=who, device_id_type=MESH
        )
        copy.start()
        copies.append(copy)

    def expand(i, c):
        rows = pl.ds(i * EXPAND_ROWS, EXPAND_ROWS)
        n = EXPAND_ROWS * 128
        cells = jnp.concatenate([lat[0, rows].reshape(n, 128), lat[1, rows].reshape(n, 128)], axis=1)
        for t in range(4):
            h = twice_gelu(dot(cells, w_expand[:, t * 256 : t * 256 + 256]).astype(BF))
            for j in range(2):
                hid[2 * t + j, pl.ds(1 + i * EXPAND_ROWS, EXPAND_ROWS), 1:9] = lanes(h, j).reshape(EXPAND_ROWS, 8, 16, 128)
        return c

    lax.fori_loop(0, 32 // EXPAND_ROWS, expand, 0)
    for copy in copies:
        copy.wait()
    zero = jnp.zeros((), BF)
    top = jnp.concatenate([halo_t[0].reshape(128, 128), halo_t[1].reshape(128, 128)], axis=1)
    bottom = jnp.concatenate([halo_b[0].reshape(128, 128), halo_b[1].reshape(128, 128)], axis=1)
    top = jnp.where(row > 0, top, zero)
    bottom = jnp.where(row < ROWS - 1, bottom, zero)
    left = jnp.concatenate([
        halo_l[...], jnp.where(row > 0, corners[0], zero), jnp.where(row < ROWS - 1, corners[2], zero)], axis=0)
    right = jnp.concatenate([
        halo_r[...], jnp.where(row > 0, corners[1], zero), jnp.where(row < ROWS - 1, corners[3], zero)], axis=0)
    left = jnp.where(col > 0, left, zero)
    right = jnp.where(col < COLS - 1, right, zero)
    around = jnp.concatenate([top, bottom, left, right], axis=0)
    for t in range(4):
        h = twice_gelu(dot(around, w_expand[:, t * 256 : t * 256 + 256]).astype(BF))
        for j in range(2):
            part = lanes(h, j)
            hid[2 * t + j, 0, 1:9] = part[:128].reshape(8, 16, 128)
            hid[2 * t + j, 33, 1:9] = part[128:256].reshape(8, 16, 128)
            hid_edge[2 * t + j] = part[256:].astype(F32)

    place_n = lax.broadcasted_iota(jnp.int32, (16, 128), 0)

    def wrap(y, c):
        place = jnp.where(y == 0, 47, jnp.where(y == 33, 48, y - 1))
        for t in range(8):
            before = pltpu.roll(hid[t, y, 8].astype(F32), 1, 0)
            hid[t, y, 0] = jnp.where(place_n == 0, hid_edge[t, pl.ds(place, 1), :], before).astype(BF)
            after = pltpu.roll(hid[t, y, 1].astype(F32), 15, 0)
            hid[t, y, 9] = jnp.where(place_n == 15, hid_edge[t, pl.ds(place + 64, 1), :], after).astype(BF)
        return c

    lax.fori_loop(0, 34, wrap, 0)

    for t in range(8):
        weights = [
            jnp.broadcast_to(taps[i // 3, i % 3 : i % 3 + 1, t * 128 : t * 128 + 128].astype(F32) * 0.5, (16, 128)).astype(BF)
            for i in range(9)
        ]

        def depthwise(y, sums):
            acc = None
            for r in range(3):
                cells = hid[t, y + r]
                for s in range(3):
                    term = weights[r * 3 + s][None] * cells[s : s + 8]
                    acc = term if acc is None else acc + term
            a = twice_gelu(acc)
            act[t, y] = a
            b = a[:4] + a[4:]
            b = b[:2] + b[2:]
            return sums + (b[0] + b[1]).astype(F32)

        sums = lax.fori_loop(0, 32, depthwise, jnp.zeros((16, 128), F32))
        total[t : t + 1, :] = jnp.sum(sums, axis=0, keepdims=True)

    ar1[row] = total[...]

    def send_row(o, c):
        pltpu.make_async_remote_copy(
            src_ref=total, dst_ref=ar1.at[row], send_sem=ar_send.at[0], recv_sem=ar_recv.at[0],
            device_id=(lax.rem(row + o, ROWS), col), device_id_type=MESH).start()
        return c

    lax.fori_loop(1, ROWS, send_row, 0)
    for load in loads[1:]:
        load.wait()
    for s in range(2):
        w_vt[s] = w_in[s, :, 512:].astype(F32).T.astype(BF)
    bias_tables(offsets, flat, bias)
    rest = ar1.at[pl.ds(0, ROWS - 1)]
    pltpu.make_async_copy(rest, rest, ar_recv.at[0]).wait()
    pltpu.make_async_copy(rest, rest, ar_send.at[0]).wait()
    ar2[col] = jnp.sum(ar1[...], axis=0)

    def send_col(o, c):
        pltpu.make_async_remote_copy(
            src_ref=ar2.at[col], dst_ref=ar2.at[col], send_sem=ar_send.at[1], recv_sem=ar_recv.at[1],
            device_id=(row, lax.rem(col + o, COLS)), device_id_type=MESH).start()
        return c

    lax.fori_loop(1, COLS, send_col, 0)
    rest = ar2.at[pl.ds(0, COLS - 1)]
    pltpu.make_async_copy(rest, rest, ar_recv.at[1]).wait()
    pltpu.make_async_copy(rest, rest, ar_send.at[1]).wait()
    total[...] = jnp.sum(ar2[...], axis=0) * (0.5 / (512 * 1024))
    squeeze = jnp.concatenate([total[i : i + 1, :] for i in range(8)], axis=1)
    squeeze = jnp.broadcast_to(squeeze, (8, 1024))
    gate = lax.dot_general(
        squeeze, down_t[...].astype(F32), NT, precision=lax.Precision.HIGHEST, preferred_element_type=F32)
    gate = gate * jax.nn.sigmoid(gate)
    excite = jax.nn.sigmoid(
        jnp.dot(gate, up[...].astype(F32), precision=lax.Precision.HIGHEST, preferred_element_type=F32))
    excite = excite.T[:, 0:1] * 0.5
    gated[...] = (w_project[...].astype(F32) * excite).astype(BF)

    weights = (gains, w_in, w_vt, w_o, w_up, w_down, bias)

    def forward(k, c):
        cells = jnp.concatenate([act[t, pl.ds(k * 8, 8)].reshape(1024, 128) for t in range(8)], axis=1)
        put(conv, pl.ds(0, 1024), dot(cells, gated[...]))
        windows = []
        for m in range(8):
            short = latent[pl.ds(k * 8, 8), m * 16 : m * 16 + 16, :].astype(F32)
            for j in range(2):
                branch = take(conv, 2 * m + j, 64, 16)
                windows.append((branch + short[:, j * 8 : j * 8 + 8].reshape(64, 256)).astype(BF).astype(F32))
        done = section_rows(jnp.concatenate(windows, axis=0), 0, *weights)
        for u in range(8):
            line = jnp.concatenate([done[n * 64 + u * 8 : n * 64 + u * 8 + 8] for n in range(16)], axis=0)
            fwd_send[k, u * 8 : u * 8 + 8] = line.astype(BF).reshape(8, 16, 256)
        pltpu.make_async_copy(fwd_send.at[k, me], fwd_recv.at[k, me], fr_sems.at[k]).start()

        def send(o, c2):
            t, who = partner(o)
            pltpu.make_async_remote_copy(
                src_ref=fwd_send.at[k, t], dst_ref=fwd_recv.at[k, me], send_sem=fs_sems.at[k], recv_sem=fr_sems.at[k],
                device_id=who, device_id_type=MESH).start()
            return c2

        lax.fori_loop(1, 64, send, 0)
        return c

    lax.fori_loop(0, BANDS, forward, 0)

    def backward(k, c):
        pltpu.make_async_copy(fwd_recv.at[k], fwd_recv.at[k], fr_sems.at[k]).wait()
        put(conv, pl.ds(0, 1024), fwd_recv[k].reshape(1024, 256).astype(F32))
        windows = jnp.concatenate([take(conv, n, 64, 16) for n in range(16)], axis=0)
        put(conv, pl.ds(0, 1024), section_rows(windows, 1, *weights))
        for t in range(64):
            back_send[k, t] = take(conv, t, 16, 64).astype(BF)
        here = out.at[k * 8 + g, pl.ds(pl.multiple_of(col * 16, 16), 16)]
        pltpu.make_async_copy(back_send.at[k, me], here, br_sems.at[k]).start()

        def send(o, c2):
            t, who = partner(o)
            pltpu.make_async_remote_copy(
                src_ref=back_send.at[k, t], dst_ref=here, send_sem=bs_sems.at[k], recv_sem=br_sems.at[k],
                device_id=who, device_id_type=MESH).start()
            return c2

        lax.fori_loop(1, 64, send, 0)
        return c

    lax.fori_loop(0, BANDS, backward, 0)

    def finish(k, c):
        band = out.at[pl.ds(k * 8, 8)]
        pltpu.make_async_copy(band, band, br_sems.at[k]).wait()
        for sems, buf in ((fs_sems, fwd_send), (bs_sems, back_send)):
            sent = buf.at[k, pl.ds(0, 63)]
            pltpu.make_async_copy(sent, sent, sems.at[k]).wait()
        return c

    lax.fori_loop(0, BANDS, finish, 0)


EXPAND_ROWS = 8


def per_device(
    latent, w_expand, w_depth, squeeze_down, squeeze_up, w_project,
    norm_gain, attend_in, attend_out, offset_bias, mixer_up, mixer_down,
):
    vmem = pl.BlockSpec(memory_space=pltpu.VMEM)
    hbm = pl.BlockSpec(memory_space=pl.ANY)
    block = (BANDS, 64, 16, 256)
    dma = pltpu.SemaphoreType.DMA
    return pl.pallas_call(
        kernel,
        out_shape=jax.ShapeDtypeStruct((32, 128, 256), BF),
        in_specs=[hbm, vmem, vmem, vmem, vmem, vmem, vmem, hbm, hbm, vmem, hbm, hbm],
        out_specs=hbm,
        scratch_shapes=[
            pltpu.VMEM((32, 128, 256), BF),
            pltpu.VMEM((2, 256, 768), BF),
            pltpu.VMEM((2, 256, 256), BF),
            pltpu.VMEM((2, 256, 1024), BF),
            pltpu.VMEM((2, 1024, 256), BF),
            pltpu.VMEM((2, 256, 256), BF),
            pltpu.VMEM((2, 2, 256, 128), F32),
            pltpu.VMEM((1024, 256), BF),
            pltpu.VMEM((2, 4096, 128), F32),
            pltpu.VMEM((2, 32, 8, 16, 128), BF),
            pltpu.VMEM((32, 256), BF),
            pltpu.VMEM((32, 256), BF),
            pltpu.VMEM((32, 256), BF),
            pltpu.VMEM((32, 256), BF),
            pltpu.VMEM((2, 8, 16, 128), BF),
            pltpu.VMEM((2, 8, 16, 128), BF),
            pltpu.VMEM((4, 16, 256), BF),
            pltpu.VMEM((8, 34, 10, 16, 128), BF),
            pltpu.VMEM((8, 128, 128), F32),
            pltpu.VMEM((8, 32, 8, 16, 128), BF),
            pltpu.VMEM((8, 128), F32),
            pltpu.VMEM((ROWS, 8, 128), F32),
            pltpu.VMEM((COLS, 8, 128), F32),
            pltpu.VMEM((2, 1024, 128), F32),
            pltpu.VMEM(block, BF),
            pltpu.VMEM(block, BF),
            pltpu.VMEM(block, BF),
            dma((5,)),
            dma((8,)),
            dma((8,)),
            dma((2,)),
            dma((2,)),
            dma((BANDS,)),
            dma((BANDS,)),
            dma((BANDS,)),
            dma((BANDS,)),
        ],
        compiler_params=pltpu.CompilerParams(collective_id=0, has_side_effects=True, vmem_limit_bytes=60 << 20),
        name="block",
    )(
        latent, w_expand, w_depth, squeeze_down.T, squeeze_up, w_project,
        norm_gain, attend_in, attend_out, offset_bias.transpose(0, 2, 1, 3), mixer_up, mixer_down,
    )


def solution(mesh):
    in_specs = (P("row", "col", None),) + (P(),) * 11
    return jax.shard_map(
        per_device, mesh=mesh, in_specs=in_specs, out_specs=P("row", "col", None), check_vma=False
    )
```

```python
import math

import jax
import jax.numpy as jnp
from jax import lax
from jax.experimental import pallas as pl
from jax.experimental.pallas import tpu as pltpu
from jax.sharding import PartitionSpec as P

MESH = pl.DeviceIdType.MESH
BF = jnp.bfloat16
F32 = jnp.float32
EPSILON = 1e-05
LOG2E = 1.4426950408889634
ROWS, COLS = 16, 8
BANDS = 4
NT = (((1,), (1,)), ((), ()))


def dot(a, b):
    return jnp.dot(a, b, preferred_element_type=F32)


def dot_nt(a, b):
    return lax.dot_general(a, b, NT, preferred_element_type=F32)


def twice_gelu(v):
    c1 = jnp.asarray(0.7978845608, v.dtype)
    c2 = jnp.asarray(0.7978845608 * 0.044715, v.dtype)
    return v + v * jnp.tanh(v * (c1 + c2 * (v * v)))


def normalise(x, gain):
    mean = jnp.sum(x, axis=-1, keepdims=True) * (1.0 / 256)
    centre = x - mean
    var = jnp.sum(centre * centre, axis=-1, keepdims=True) * (1.0 / 256)
    return (centre * lax.rsqrt(var + EPSILON) * gain).astype(BF)


def put(ref, rows, value):
    ref[0, rows, :] = value[:, :128]
    ref[1, rows, :] = value[:, 128:]


def take(ref, start, count, stride):
    rows = pl.ds(start, count, stride=stride)
    return jnp.concatenate([ref[0, rows, :], ref[1, rows, :]], axis=1)


def lanes(value, t):
    return value[:, t * 128 : t * 128 + 128]


def attention_pair(q2, k2, vt2, bias, s):
    lane = lax.broadcasted_iota(jnp.int32, (64, 256), 1)
    lane_head = lax.rem(lane, 128) // 32
    first = lax.broadcasted_iota(jnp.int32, (32, 128), 1) < 64
    first_out = lax.broadcasted_iota(jnp.int32, (128, 128), 1) < 64
    zero = jnp.zeros((), BF)
    z = jnp.zeros((64, 128), BF)
    z32 = jnp.zeros((32, 128), BF)
    scale = LOG2E / math.sqrt(32)
    out = []
    for half in range(2):
        f = slice(half * 128, half * 128 + 128)
        qh, kh, vh = q2[:, f], k2[:, f], vt2[f, :]
        q_block = jnp.concatenate(
            [jnp.concatenate([qh[:64], z], axis=1), jnp.concatenate([z, qh[64:]], axis=1)], axis=0)
        k_both = jnp.concatenate([kh[:64], kh[64:]], axis=1)
        k_block = jnp.concatenate([jnp.where(lane_head == h, k_both, zero) for h in range(4)], axis=0)
        scores = dot_nt(k_block, q_block) * scale + bias[s, half]
        scores = scores.reshape(4, 64, 128)
        raised = jnp.exp2(scores - jnp.max(scores, axis=1, keepdims=True))
        inverse = 1.0 / jnp.sum(raised, axis=1, keepdims=True)
        weights = raised.astype(BF).reshape(256, 128)
        swapped = jnp.concatenate([vh[:, 64:], vh[:, :64]], axis=1)
        lhs = []
        for w in range(2):
            for h in range(4):
                source = (vh if h % 2 == w else swapped)[h * 32 : h * 32 + 32]
                kept = jnp.where(first, source, zero) if h % 2 == 0 else jnp.where(first, zero, source)
                lhs.append(jnp.concatenate([kept, z32] if h < 2 else [z32, kept], axis=1))
        mixed = dot(jnp.concatenate(lhs, axis=0), weights)
        mixed = jnp.where(first_out, mixed[:128], mixed[128:]).reshape(4, 32, 128) * inverse
        out.append(mixed.reshape(128, 128))
    return jnp.concatenate(out, axis=0)


def section_rows(x, s, gains, w_in, w_vt, w_o, w_up, w_down, bias):
    n = x.shape[0]
    normed = normalise(x, gains[s, 0:1])
    qk = dot(normed, w_in[s, :, :512]).astype(BF)
    vt = dot_nt(w_vt[s], normed).astype(BF)
    mixes = []
    for p in range(n // 128):
        r = slice(p * 128, p * 128 + 128)
        mixed = attention_pair(qk[r, :256], qk[r, 256:], vt[:, r], bias, s)
        mixes.append(mixed.T.astype(BF))
    closed = []
    for i in range(0, n // 128, 4):
        mix = jnp.concatenate(mixes[i : i + 4], axis=0)
        closed.append((x[i * 128 : i * 128 + 512] + dot(mix, w_o[s])).astype(BF).astype(F32))
    normed = jnp.concatenate([normalise(a, gains[s, 1:2]) for a in closed], axis=0)
    attended = jnp.concatenate(closed, axis=0)
    low = []
    for r in range(n // 256):
        rows = normed[r * 256 : r * 256 + 256]
        up = [twice_gelu(dot(rows, w_up[s, :, t * 256 : t * 256 + 256]).astype(BF)) for t in range(4)]
        low.append(dot(jnp.concatenate(up, axis=1), w_down[s]))
    return attended + 0.5 * jnp.concatenate(low, axis=0)


def bias_tables(offsets, flat, bias):
    pad = jnp.zeros((8, 113), F32)
    parts = []
    for s in range(2):
        for tile in range(2):
            acc = jnp.zeros((8, 128), F32)
            for r in range(tile * 8, min(tile * 8 + 8, 15)):
                row = jnp.concatenate([offsets[s, r] * LOG2E, pad], axis=1)
                shift = (r - tile * 8) * 16
                acc = acc + (pltpu.roll(row, shift, 1) if shift else row)
            parts.append(acc)
    table = jnp.concatenate(
        [jnp.concatenate(parts[:2], axis=1), jnp.concatenate(parts[2:], axis=1)], axis=0)
    high = table.astype(BF)
    rest = table - high.astype(F32)
    middle = rest.astype(BF)
    low = (rest - middle.astype(F32)).astype(BF)
    source = lax.broadcasted_iota(jnp.int32, (256, 128), 0)
    target = lax.broadcasted_iota(jnp.int32, (256, 128), 1)
    same_row = source // 16 == target // 8
    for key_col in range(8):
        pick = same_row & (lax.rem(source, 16) == lax.rem(target, 8) + (7 - key_col))
        pick = jnp.where(pick, 1.0, 0.0).astype(BF)
        flat[0, key_col * 16 : key_col * 16 + 16, :] = dot(high, pick) + dot(middle, pick) + dot(low, pick)
    left = lax.broadcasted_iota(jnp.int32, (8, 128), 1) < 64
    for s in range(2):
        for h in range(8):
            block = flat[0, pl.ds(s * 8 + h, 8, stride=16), :]
            for key_row in range(8):
                first = pltpu.roll(block, (128 - (7 - key_row) * 8) % 128, 1) if key_row < 7 else block
                both = jnp.where(left, first, pltpu.roll(first, 64, 1))
                start = (h % 4) * 64 + key_row * 8
                bias[s, h // 4, start : start + 8, :] = both


def kernel(
    latent_hbm, w_expand, taps, down_t, up, w_project, gains, w_in_hbm, w_o_hbm, offsets, w_up_hbm, w_down_hbm,
    out,
    latent, w_in, w_o, w_up, w_down, w_vt, bias, gated,
    flat, lat, edge_l, edge_r, halo_l, halo_r, halo_t, halo_b, corners, hid, hid_edge, act,
    total, ar1, ar2, conv, fwd_send, fwd_recv, back_send,
    load_sems, send_sems, recv_sems, ar_send, ar_recv, fs_sems, fr_sems, bs_sems, br_sems,
):
    row, col = lax.axis_index("row"), lax.axis_index("col")
    core, g = lax.rem(row, 2), row // 2
    me = g * 8 + col
    up_row, dn_row = lax.rem(row + ROWS - 1, ROWS), lax.rem(row + 1, ROWS)
    lf, rt = lax.rem(col + COLS - 1, COLS), lax.rem(col + 1, COLS)
    z, ylo, yhi, x = g // 2, lax.rem(g, 2), col // 4, lax.rem(col, 4)
    y = yhi * 2 + ylo

    xs = [lax.rem(x + d, 4) for d in range(4)]
    ys = [lax.rem(y + d, 4) for d in range(4)]
    zs = [lax.rem(z + d, 4) for d in range(4)]
    groups = [[zs[dz] * 2 + lax.rem(ys[dy], 2) for dy in range(4)] for dz in range(4)]
    columns = [[(ys[dy] // 2) * 4 + xs[dx] for dx in range(4)] for dy in range(4)]

    parity = lax.rem(x + y + z, 2)
    depths = [zs[dz] * 16 for dz in range(4)]
    heights = [(ys[dy] // 2) * 8 + lax.rem(ys[dy], 2) * 2 for dy in range(4)]
    halves = [xs[dx] // 2 for dx in range(4)]
    own = z * 16 + (y // 2) * 8 + parity * 4 + lax.rem(y, 2) * 2 + x // 2

    def exchange(source, target, send_sem, recv_sem, offsets):
        for dx, dy, dz in offsets:
            group, column = groups[dz][dy], columns[dy][dx]
            pltpu.make_async_remote_copy(
                src_ref=source(group * 8 + column, depths[dz] + heights[dy] + halves[dx]), dst_ref=target,
                send_sem=send_sem, recv_sem=recv_sem, device_id=(group * 2 + core, column), device_id_type=MESH).start()

    loads = [
        pltpu.make_async_copy(src, dst, load_sems.at[i])
        for i, (src, dst) in enumerate(
            ((latent_hbm, latent), (w_in_hbm, w_in), (w_o_hbm, w_o), (w_up_hbm, w_up), (w_down_hbm, w_down)))
    ]
    for load in loads:
        load.start()

    barrier = pltpu.get_barrier_semaphore()
    for who in ((row, lf), (row, rt), (up_row, col), (dn_row, col), (up_row, lf), (up_row, rt), (dn_row, lf), (dn_row, rt)):
        pl.semaphore_signal(barrier, inc=1, device_id=who, device_id_type=MESH)

    for dx, dy, dz in ORDER:
        pl.semaphore_signal(barrier, inc=1, device_id=(groups[dz][dy] * 2 + core, columns[dy][dx]), device_id_type=MESH)
    loads[0].wait()

    edge_l[...] = latent[:, :16, :].astype(F32)[:, 0, :].astype(BF)
    edge_r[...] = latent[:, 112:, :].astype(F32)[:, 15, :].astype(BF)
    pl.semaphore_wait(barrier, 8 + 63)
    first, last = pl.ds(0, 16), pl.ds(16, 16)
    moves = (
        (edge_l, halo_r, (row, lf)),
        (edge_r, halo_l, (row, rt)),
        (latent.at[0], halo_b, (up_row, col)),
        (latent.at[31], halo_t, (dn_row, col)),
        (edge_l.at[first], corners.at[3], (up_row, lf)),
        (edge_r.at[first], corners.at[2], (up_row, rt)),
        (edge_l.at[last], corners.at[1], (dn_row, lf)),
        (edge_r.at[last], corners.at[0], (dn_row, rt)),
    )
    copies = []
    for i, (src, dst, who) in enumerate(moves):
        copy = pltpu.make_async_remote_copy(
            src_ref=src, dst_ref=dst, send_sem=send_sems.at[i], recv_sem=recv_sems.at[i], device_id=who, device_id_type=MESH
        )
        copy.start()
        copies.append(copy)

    def spread(y, c):
        put(flat, pl.ds(pl.multiple_of(y * 128, 128), 128), latent[y].astype(F32))
        for v in range(8):
            for j in range(2):
                lat[j, y, v] = flat[j, pl.ds(y * 128 + v, 16, stride=8), :].astype(BF)
        return c

    lax.fori_loop(0, 32, spread, 0)
    def expand(i, c):
        rows = pl.ds(i * EXPAND_ROWS, EXPAND_ROWS)
        n = EXPAND_ROWS * 128
        cells = jnp.concatenate([lat[0, rows].reshape(n, 128), lat[1, rows].reshape(n, 128)], axis=1)
        for t in range(4):
            h = twice_gelu(dot(cells, w_expand[:, t * 256 : t * 256 + 256]).astype(BF))
            for j in range(2):
                hid[2 * t + j, pl.ds(1 + i * EXPAND_ROWS, EXPAND_ROWS), 1:9] = lanes(h, j).reshape(EXPAND_ROWS, 8, 16, 128)
        return c

    lax.fori_loop(0, 32 // EXPAND_ROWS, expand, 0)
    for copy in copies:
        copy.wait()
    zero = jnp.zeros((), BF)
    edge_rows = []
    for i, (halo, inside) in enumerate(((halo_t, row > 0), (halo_b, row < ROWS - 1))):
        put(flat, pl.ds(i * 128, 128), halo[...].astype(F32))
        cells = jnp.concatenate([take(flat, i * 128 + v, 16, 8) for v in range(8)], axis=0)
        edge_rows.append(jnp.where(inside, cells, 0.0).astype(BF))
    left = jnp.concatenate([
        halo_l[...], jnp.where(row > 0, corners[0], zero), jnp.where(row < ROWS - 1, corners[2], zero)], axis=0)
    right = jnp.concatenate([
        halo_r[...], jnp.where(row > 0, corners[1], zero), jnp.where(row < ROWS - 1, corners[3], zero)], axis=0)
    left = jnp.where(col > 0, left, zero)
    right = jnp.where(col < COLS - 1, right, zero)
    around = jnp.concatenate(edge_rows + [left, right], axis=0)
    for t in range(4):
        h = twice_gelu(dot(around, w_expand[:, t * 256 : t * 256 + 256]).astype(BF))
        for j in range(2):
            part = lanes(h, j)
            hid[2 * t + j, 0, 1:9] = part[:128].reshape(8, 16, 128)
            hid[2 * t + j, 33, 1:9] = part[128:256].reshape(8, 16, 128)
            hid_edge[2 * t + j] = part[256:].astype(F32)

    place_n = lax.broadcasted_iota(jnp.int32, (16, 128), 0)

    def wrap(i, c):
        for y in (2 * i, 2 * i + 1):
            place = jnp.where(y == 0, 47, jnp.where(y == 33, 48, y - 1))
            for t in range(8):
                before = pltpu.roll(hid[t, y, 8].astype(F32), 1, 0)
                hid[t, y, 0] = jnp.where(place_n == 0, hid_edge[t, pl.ds(place, 1), :], before).astype(BF)
                after = pltpu.roll(hid[t, y, 1].astype(F32), 15, 0)
                hid[t, y, 9] = jnp.where(place_n == 15, hid_edge[t, pl.ds(place + 64, 1), :], after).astype(BF)
        return c

    lax.fori_loop(0, 17, wrap, 0)

    for t in range(8):
        weights = [
            jnp.broadcast_to(taps[i // 3, i % 3 : i % 3 + 1, t * 128 : t * 128 + 128].astype(F32) * 0.5, (16, 128)).astype(BF)
            for i in range(9)
        ]

        def depthwise(i, sums):
            y = i * DEPTH_ROWS
            accs = [None] * DEPTH_ROWS
            for r in range(DEPTH_ROWS + 2):
                cells = hid[t, y + r]
                for q in range(max(0, r - 2), min(DEPTH_ROWS, r + 1)):
                    for s in range(3):
                        term = weights[(r - q) * 3 + s][None] * cells[s : s + 8]
                        accs[q] = term if accs[q] is None else accs[q] + term
                if r >= 2:
                    a = twice_gelu(accs[r - 2])
                    act[t, y + r - 2] = a
                    b = a[:4] + a[4:]
                    b = b[:2] + b[2:]
                    sums = sums + (b[0] + b[1]).astype(F32)
            return sums

        sums = lax.fori_loop(0, 32 // DEPTH_ROWS, depthwise, jnp.zeros((16, 128), F32))
        total[t : t + 1, :] = jnp.sum(sums, axis=0, keepdims=True)

    ar1[me] = total[...]
    exchange(lambda device, share: total, ar1.at[me], ar_send.at[0], ar_recv.at[0], ORDER)
    for load in loads[1:]:
        load.wait()
    for s in range(2):
        w_vt[s] = w_in[s, :, 512:].astype(F32).T.astype(BF)
    bias_tables(offsets, flat, bias)
    rest = ar1.at[pl.ds(0, 63)]
    pltpu.make_async_copy(rest, rest, ar_recv.at[0]).wait()
    ar2[core] = jnp.sum(ar1[...], axis=0)
    sibling = pltpu.make_async_remote_copy(
        src_ref=ar2.at[core], dst_ref=ar2.at[core], send_sem=ar_send.at[1], recv_sem=ar_recv.at[1],
        device_id=(g * 2 + 1 - core, col), device_id_type=MESH)
    sibling.start()
    sibling.wait()
    mean = jnp.sum(ar2[...], axis=0) * (0.5 / (512 * 1024))
    squeeze = jnp.concatenate([mean[i : i + 1, :] for i in range(8)], axis=1)
    squeeze = jnp.broadcast_to(squeeze, (8, 1024))
    gate = lax.dot_general(
        squeeze, down_t[...].astype(F32), NT, precision=lax.Precision.HIGHEST, preferred_element_type=F32)
    gate = gate * jax.nn.sigmoid(gate)
    excite = jax.nn.sigmoid(
        jnp.dot(gate, up[...].astype(F32), precision=lax.Precision.HIGHEST, preferred_element_type=F32))
    excite = excite.T[:, 0:1] * 0.5
    gated[...] = (w_project[...].astype(F32) * excite).astype(BF)

    weights = (gains, w_in, w_vt, w_o, w_up, w_down, bias)

    def forward(k, c):
        cells = jnp.concatenate([act[t, pl.ds(k * 8, 8)].reshape(1024, 128) for t in range(8)], axis=1)
        put(conv, pl.ds(0, 1024), dot(cells, gated[...]))
        windows = []
        for m in range(8):
            short = latent[pl.ds(k * 8, 8), m * 16 : m * 16 + 16, :].astype(F32)
            for j in range(2):
                branch = take(conv, 2 * m + j, 64, 16)
                windows.append((branch + short[:, j * 8 : j * 8 + 8].reshape(64, 256)).astype(BF).astype(F32))
        done = section_rows(jnp.concatenate(windows, axis=0), 0, *weights)
        for u in range(8):
            line = jnp.concatenate([done[n * 64 + u * 8 : n * 64 + u * 8 + 8] for n in range(16)], axis=0)
            fwd_send[k, u * 8 : u * 8 + 8] = line.astype(BF).reshape(8, 16, 256)
        pltpu.make_async_copy(fwd_send.at[k, me], fwd_recv.at[k, me], fr_sems.at[k]).start()

        exchange(lambda device, share: fwd_send.at[k, device], fwd_recv.at[k, me], fs_sems.at[k], fr_sems.at[k], ORDER)
        return c

    lax.fori_loop(0, BANDS, forward, 0)

    def backward(k, c):
        pltpu.make_async_copy(fwd_recv.at[k], fwd_recv.at[k], fr_sems.at[k]).wait()
        put(conv, pl.ds(0, 1024), fwd_recv[k].reshape(1024, 256).astype(F32))
        windows = jnp.concatenate([take(conv, n, 64, 16) for n in range(16)], axis=0)
        put(conv, pl.ds(0, 1024), section_rows(windows, 1, *weights))
        for t in range(64):
            back_send[k, t] = take(conv, t, 16, 64).astype(BF)
        here = out.at[k * 16 + g * 2 + col // 4, pl.ds(pl.multiple_of(lax.rem(col, 4) * 16, 16), 16)]
        pltpu.make_async_copy(back_send.at[k, me], here, br_sems.at[k]).start()

        exchange(lambda device, share: back_send.at[k, device], here, bs_sems.at[k], br_sems.at[k], ORDER)
        return c

    lax.fori_loop(0, BANDS, backward, 0)

    def finish(k, c):
        band = out.at[pl.ds(k * 16, 16)]
        pltpu.make_async_copy(band, band, br_sems.at[k]).wait()
        for sems, buf in ((fs_sems, fwd_send), (bs_sems, back_send)):
            sent = buf.at[k, pl.ds(0, 63)]
            pltpu.make_async_copy(sent, sent, sems.at[k]).wait()
        return c

    lax.fori_loop(0, BANDS, finish, 0)
    pltpu.make_async_copy(rest, rest, ar_send.at[0]).wait()


EXPAND_ROWS = 8
DEPTH_ROWS = 4


def hops(offset):
    return sum(min(d, 4 - d) for d in offset)


ORDER = sorted(
    ((dx, dy, dz) for dx in range(4) for dy in range(4) for dz in range(4) if (dx, dy, dz) != (0, 0, 0)),
    key=lambda o: (-hops(o), min(o, tuple(-d % 4 for d in o))[::-1]),
)


def per_device(
    latent, w_expand, w_depth, squeeze_down, squeeze_up, w_project,
    norm_gain, attend_in, attend_out, offset_bias, mixer_up, mixer_down,
):
    vmem = pl.BlockSpec(memory_space=pltpu.VMEM)
    hbm = pl.BlockSpec(memory_space=pl.ANY)
    block = (BANDS, 64, 16, 256)
    dma = pltpu.SemaphoreType.DMA
    return pl.pallas_call(
        kernel,
        out_shape=jax.ShapeDtypeStruct((64, 64, 256), BF),
        in_specs=[hbm, vmem, vmem, vmem, vmem, vmem, vmem, hbm, hbm, vmem, hbm, hbm],
        out_specs=hbm,
        scratch_shapes=[
            pltpu.VMEM((32, 128, 256), BF),
            pltpu.VMEM((2, 256, 768), BF),
            pltpu.VMEM((2, 256, 256), BF),
            pltpu.VMEM((2, 256, 1024), BF),
            pltpu.VMEM((2, 1024, 256), BF),
            pltpu.VMEM((2, 256, 256), BF),
            pltpu.VMEM((2, 2, 256, 128), F32),
            pltpu.VMEM((1024, 256), BF),
            pltpu.VMEM((2, 4096, 128), F32),
            pltpu.VMEM((2, 32, 8, 16, 128), BF),
            pltpu.VMEM((32, 256), BF),
            pltpu.VMEM((32, 256), BF),
            pltpu.VMEM((32, 256), BF),
            pltpu.VMEM((32, 256), BF),
            pltpu.VMEM((128, 256), BF),
            pltpu.VMEM((128, 256), BF),
            pltpu.VMEM((4, 16, 256), BF),
            pltpu.VMEM((8, 34, 10, 16, 128), BF),
            pltpu.VMEM((8, 128, 128), F32),
            pltpu.VMEM((8, 32, 8, 16, 128), BF),
            pltpu.VMEM((8, 128), F32),
            pltpu.VMEM((64, 8, 128), F32),
            pltpu.VMEM((2, 8, 128), F32),
            pltpu.VMEM((2, 1024, 128), F32),
            pltpu.VMEM(block, BF),
            pltpu.VMEM(block, BF),
            pltpu.VMEM(block, BF),
            dma((5,)),
            dma((8,)),
            dma((8,)),
            dma((2,)),
            dma((2,)),
            dma((BANDS,)),
            dma((BANDS,)),
            dma((BANDS,)),
            dma((BANDS,)),
        ],
        compiler_params=pltpu.CompilerParams(collective_id=0, has_side_effects=True, vmem_limit_bytes=46 << 20),
        name="block",
    )(*(pltpu.with_memory_space_constraint(a, pltpu.HBM) for a in (
        latent, w_expand, w_depth, squeeze_down.T, squeeze_up, w_project,
        norm_gain, attend_in, attend_out, offset_bias.transpose(0, 2, 1, 3), mixer_up, mixer_down,
    ))).reshape(32, 128, 256)


def solution(mesh):
    in_specs = (P("row", "col", None),) + (P(),) * 11
    return jax.shard_map(
        per_device, mesh=mesh, in_specs=in_specs, out_specs=P("row", "col", None), check_vma=False
    )
```

```python
import math

import jax
import jax.numpy as jnp
from jax import lax
from jax.experimental import pallas as pl
from jax.experimental.pallas import tpu as pltpu
from jax.sharding import PartitionSpec as P

MESH = pl.DeviceIdType.MESH
BF = jnp.bfloat16
F32 = jnp.float32
EPSILON = 1e-05
LOG2E = 1.4426950408889634
ROWS, COLS = 16, 8
BANDS = 4
NT = (((1,), (1,)), ((), ()))


def dot(a, b):
    return jnp.dot(a, b, preferred_element_type=F32)


def dot_nt(a, b):
    return lax.dot_general(a, b, NT, preferred_element_type=F32)


def twice_gelu(v):
    c1 = jnp.asarray(0.7978845608, v.dtype)
    c2 = jnp.asarray(0.7978845608 * 0.044715, v.dtype)
    return v + v * jnp.tanh(v * (c1 + c2 * (v * v)))


def normalise(x, gain):
    mean = jnp.sum(x, axis=-1, keepdims=True) * (1.0 / 256)
    centre = x - mean
    var = jnp.sum(centre * centre, axis=-1, keepdims=True) * (1.0 / 256)
    return (centre * lax.rsqrt(var + EPSILON) * gain).astype(BF)


def put(ref, rows, value):
    ref[0, rows, :] = value[:, :128]
    ref[1, rows, :] = value[:, 128:]


def take(ref, start, count, stride):
    rows = pl.ds(start, count, stride=stride)
    return jnp.concatenate([ref[0, rows, :], ref[1, rows, :]], axis=1)


def lanes(value, t):
    return value[:, t * 128 : t * 128 + 128]


def attention_pair(q2, k2, vt2, bias, s):
    lane = lax.broadcasted_iota(jnp.int32, (64, 256), 1)
    lane_head = lax.rem(lane, 128) // 32
    first = lax.broadcasted_iota(jnp.int32, (32, 128), 1) < 64
    first_out = lax.broadcasted_iota(jnp.int32, (128, 128), 1) < 64
    zero = jnp.zeros((), BF)
    z = jnp.zeros((64, 128), BF)
    z32 = jnp.zeros((32, 128), BF)
    scale = LOG2E / math.sqrt(32)
    out = []
    for half in range(2):
        f = slice(half * 128, half * 128 + 128)
        qh, kh, vh = q2[:, f], k2[:, f], vt2[f, :]
        q_block = jnp.concatenate(
            [jnp.concatenate([qh[:64], z], axis=1), jnp.concatenate([z, qh[64:]], axis=1)], axis=0)
        k_both = jnp.concatenate([kh[:64], kh[64:]], axis=1)
        k_block = jnp.concatenate([jnp.where(lane_head == h, k_both, zero) for h in range(4)], axis=0)
        scores = dot_nt(k_block, q_block) * scale + bias[s, half]
        scores = scores.reshape(4, 64, 128)
        raised = jnp.exp2(scores - jnp.max(scores, axis=1, keepdims=True))
        inverse = 1.0 / jnp.sum(raised, axis=1, keepdims=True)
        weights = raised.astype(BF).reshape(256, 128)
        swapped = jnp.concatenate([vh[:, 64:], vh[:, :64]], axis=1)
        lhs = []
        for w in range(2):
            for h in range(4):
                source = (vh if h % 2 == w else swapped)[h * 32 : h * 32 + 32]
                kept = jnp.where(first, source, zero) if h % 2 == 0 else jnp.where(first, zero, source)
                lhs.append(jnp.concatenate([kept, z32] if h < 2 else [z32, kept], axis=1))
        mixed = dot(jnp.concatenate(lhs, axis=0), weights)
        mixed = jnp.where(first_out, mixed[:128], mixed[128:]).reshape(4, 32, 128) * inverse
        out.append(mixed.reshape(128, 128))
    return jnp.concatenate(out, axis=0)


def section_rows(x, s, gains, w_in, w_vt, w_o, w_up, w_down, bias):
    n = x.shape[0]
    normed = normalise(x, gains[s, 0:1])
    qk = dot(normed, w_in[s, :, :512]).astype(BF)
    vt = dot_nt(w_vt[s], normed).astype(BF)
    mixes = []
    for p in range(n // 128):
        r = slice(p * 128, p * 128 + 128)
        mixed = attention_pair(qk[r, :256], qk[r, 256:], vt[:, r], bias, s)
        mixes.append(mixed.T.astype(BF))
    closed = []
    for i in range(0, n // 128, 4):
        mix = jnp.concatenate(mixes[i : i + 4], axis=0)
        closed.append((x[i * 128 : i * 128 + 512] + dot(mix, w_o[s])).astype(BF).astype(F32))
    normed = jnp.concatenate([normalise(a, gains[s, 1:2]) for a in closed], axis=0)
    attended = jnp.concatenate(closed, axis=0)
    low = []
    for r in range(n // 256):
        rows = normed[r * 256 : r * 256 + 256]
        up = [twice_gelu(dot(rows, w_up[s, :, t * 256 : t * 256 + 256]).astype(BF)) for t in range(4)]
        low.append(dot(jnp.concatenate(up, axis=1), w_down[s]))
    return attended + 0.5 * jnp.concatenate(low, axis=0)


def bias_tables(offsets, flat, bias):
    pad = jnp.zeros((8, 113), F32)
    parts = []
    for s in range(2):
        for tile in range(2):
            acc = jnp.zeros((8, 128), F32)
            for r in range(tile * 8, min(tile * 8 + 8, 15)):
                row = jnp.concatenate([offsets[s, r] * LOG2E, pad], axis=1)
                shift = (r - tile * 8) * 16
                acc = acc + (pltpu.roll(row, shift, 1) if shift else row)
            parts.append(acc)
    table = jnp.concatenate(
        [jnp.concatenate(parts[:2], axis=1), jnp.concatenate(parts[2:], axis=1)], axis=0)
    high = table.astype(BF)
    rest = table - high.astype(F32)
    middle = rest.astype(BF)
    low = (rest - middle.astype(F32)).astype(BF)
    source = lax.broadcasted_iota(jnp.int32, (256, 128), 0)
    target = lax.broadcasted_iota(jnp.int32, (256, 128), 1)
    same_row = source // 16 == target // 8
    for key_col in range(8):
        pick = same_row & (lax.rem(source, 16) == lax.rem(target, 8) + (7 - key_col))
        pick = jnp.where(pick, 1.0, 0.0).astype(BF)
        flat[0, key_col * 16 : key_col * 16 + 16, :] = dot(high, pick) + dot(middle, pick) + dot(low, pick)
    left = lax.broadcasted_iota(jnp.int32, (8, 128), 1) < 64
    for s in range(2):
        for h in range(8):
            block = flat[0, pl.ds(s * 8 + h, 8, stride=16), :]
            for key_row in range(8):
                first = pltpu.roll(block, (128 - (7 - key_row) * 8) % 128, 1) if key_row < 7 else block
                both = jnp.where(left, first, pltpu.roll(first, 64, 1))
                start = (h % 4) * 64 + key_row * 8
                bias[s, h // 4, start : start + 8, :] = both


def kernel(
    latent_hbm, w_expand_hbm, taps_hbm, down_hbm, up_hbm, w_project_hbm, gains_hbm, w_in_hbm, w_o_hbm, offsets_hbm,
    w_up_hbm, w_down_hbm,
    out,
    side_l, side_r, latent, w_expand, taps, down_t, up, w_project, gains, w_in, w_o, offsets, w_up, w_down,
    w_vt, bias, gated,
    flat, lat, edge_l, edge_r, halo_l, halo_r, halo_t, halo_b, corners, hid, hid_edge, act,
    total, ar1, ar2, conv, fwd_send, fwd_recv, back_send,
    load_sems, send_sems, recv_sems, ar_send, ar_recv, fs_sems, fr_sems, bs_sems, br_sems,
):
    row, col = lax.axis_index("row"), lax.axis_index("col")
    core, g = lax.rem(row, 2), row // 2
    me = g * 8 + col
    up_row, dn_row = lax.rem(row + ROWS - 1, ROWS), lax.rem(row + 1, ROWS)
    lf, rt = lax.rem(col + COLS - 1, COLS), lax.rem(col + 1, COLS)
    z, ylo, yhi, x = g // 2, lax.rem(g, 2), col // 4, lax.rem(col, 4)
    y = yhi * 2 + ylo

    xs = [lax.rem(x + d, 4) for d in range(4)]
    ys = [lax.rem(y + d, 4) for d in range(4)]
    zs = [lax.rem(z + d, 4) for d in range(4)]
    groups = [[zs[dz] * 2 + lax.rem(ys[dy], 2) for dy in range(4)] for dz in range(4)]
    columns = [[(ys[dy] // 2) * 4 + xs[dx] for dx in range(4)] for dy in range(4)]

    parity = lax.rem(x + y + z, 2)
    depths = [zs[dz] * 16 for dz in range(4)]
    heights = [(ys[dy] // 2) * 8 + lax.rem(ys[dy], 2) * 2 for dy in range(4)]
    halves = [xs[dx] // 2 for dx in range(4)]
    own = z * 16 + (y // 2) * 8 + parity * 4 + lax.rem(y, 2) * 2 + x // 2

    def exchange(source, target, send_sem, recv_sem, offsets):
        for dx, dy, dz in offsets:
            group, column = groups[dz][dy], columns[dy][dx]
            pltpu.make_async_remote_copy(
                src_ref=source(group * 8 + column, depths[dz] + heights[dy] + halves[dx]), dst_ref=target,
                send_sem=send_sem, recv_sem=recv_sem, device_id=(group * 2 + core, column), device_id_type=MESH).start()

    pairs = (
        (latent_hbm.at[:, pl.ds(0, 16), :], side_l), (latent_hbm.at[:, pl.ds(112, 16), :], side_r),
        (latent_hbm, latent), (w_expand_hbm, w_expand), (taps_hbm, taps), (down_hbm, down_t), (up_hbm, up),
        (w_project_hbm, w_project), (gains_hbm, gains), (w_in_hbm, w_in), (w_o_hbm, w_o), (offsets_hbm, offsets),
        (w_up_hbm, w_up), (w_down_hbm, w_down),
    )
    loads = [pltpu.make_async_copy(src, dst, load_sems.at[i]) for i, (src, dst) in enumerate(pairs)]
    for load in loads:
        load.start()

    barrier = pltpu.get_barrier_semaphore()
    for who in ((row, lf), (row, rt), (up_row, col), (dn_row, col), (up_row, lf), (up_row, rt), (dn_row, lf), (dn_row, rt)):
        pl.semaphore_signal(barrier, inc=1, device_id=who, device_id_type=MESH)

    for dx, dy, dz in ORDER:
        pl.semaphore_signal(barrier, inc=1, device_id=(groups[dz][dy] * 2 + core, columns[dy][dx]), device_id_type=MESH)
    loads[0].wait()
    loads[1].wait()

    edge_l[...] = side_l[...].astype(F32)[:, 0, :].astype(BF)
    edge_r[...] = side_r[...].astype(F32)[:, 15, :].astype(BF)
    pl.semaphore_wait(barrier, 8 + 63)
    first, last = pl.ds(0, 16), pl.ds(16, 16)
    moves = (
        (edge_l, halo_r, (row, lf)),
        (edge_r, halo_l, (row, rt)),
        (latent_hbm.at[0], halo_b, (up_row, col)),
        (latent_hbm.at[31], halo_t, (dn_row, col)),
        (edge_l.at[first], corners.at[3], (up_row, lf)),
        (edge_r.at[first], corners.at[2], (up_row, rt)),
        (edge_l.at[last], corners.at[1], (dn_row, lf)),
        (edge_r.at[last], corners.at[0], (dn_row, rt)),
    )
    copies = []
    for i, (src, dst, who) in enumerate(moves):
        copy = pltpu.make_async_remote_copy(
            src_ref=src, dst_ref=dst, send_sem=send_sems.at[i], recv_sem=recv_sems.at[i], device_id=who, device_id_type=MESH
        )
        copy.start()
        copies.append(copy)

    loads[2].wait()

    def spread(y, c):
        put(flat, pl.ds(pl.multiple_of(y * 128, 128), 128), latent[y].astype(F32))
        for v in range(8):
            for j in range(2):
                lat[j, y, v] = flat[j, pl.ds(y * 128 + v, 16, stride=8), :].astype(BF)
        return c

    lax.fori_loop(0, 32, spread, 0)
    def expand(i, c):
        rows = pl.ds(i * EXPAND_ROWS, EXPAND_ROWS)
        n = EXPAND_ROWS * 128
        cells = jnp.concatenate([lat[0, rows].reshape(n, 128), lat[1, rows].reshape(n, 128)], axis=1)
        for t in range(4):
            h = twice_gelu(dot(cells, w_expand[:, t * 256 : t * 256 + 256]).astype(BF))
            for j in range(2):
                hid[2 * t + j, pl.ds(1 + i * EXPAND_ROWS, EXPAND_ROWS), 1:9] = lanes(h, j).reshape(EXPAND_ROWS, 8, 16, 128)
        return c

    loads[3].wait()
    lax.fori_loop(0, 32 // EXPAND_ROWS, expand, 0)
    for copy in copies:
        copy.wait()
    zero = jnp.zeros((), BF)
    edge_rows = []
    for i, (halo, inside) in enumerate(((halo_t, row > 0), (halo_b, row < ROWS - 1))):
        put(flat, pl.ds(i * 128, 128), halo[...].astype(F32))
        cells = jnp.concatenate([take(flat, i * 128 + v, 16, 8) for v in range(8)], axis=0)
        edge_rows.append(jnp.where(inside, cells, 0.0).astype(BF))
    left = jnp.concatenate([
        halo_l[...], jnp.where(row > 0, corners[0], zero), jnp.where(row < ROWS - 1, corners[2], zero)], axis=0)
    right = jnp.concatenate([
        halo_r[...], jnp.where(row > 0, corners[1], zero), jnp.where(row < ROWS - 1, corners[3], zero)], axis=0)
    left = jnp.where(col > 0, left, zero)
    right = jnp.where(col < COLS - 1, right, zero)
    around = jnp.concatenate(edge_rows + [left, right], axis=0)
    for t in range(4):
        h = twice_gelu(dot(around, w_expand[:, t * 256 : t * 256 + 256]).astype(BF))
        for j in range(2):
            part = lanes(h, j)
            hid[2 * t + j, 0, 1:9] = part[:128].reshape(8, 16, 128)
            hid[2 * t + j, 33, 1:9] = part[128:256].reshape(8, 16, 128)
            hid_edge[2 * t + j] = part[256:].astype(F32)

    loads[4].wait()
    place_n = lax.broadcasted_iota(jnp.int32, (16, 128), 0)

    def wrap(i, c):
        for y in (2 * i, 2 * i + 1):
            place = jnp.where(y == 0, 47, jnp.where(y == 33, 48, y - 1))
            for t in range(8):
                before = pltpu.roll(hid[t, y, 8].astype(F32), 1, 0)
                hid[t, y, 0] = jnp.where(place_n == 0, hid_edge[t, pl.ds(place, 1), :], before).astype(BF)
                after = pltpu.roll(hid[t, y, 1].astype(F32), 15, 0)
                hid[t, y, 9] = jnp.where(place_n == 15, hid_edge[t, pl.ds(place + 64, 1), :], after).astype(BF)
        return c

    lax.fori_loop(0, 17, wrap, 0)

    for t in range(8):
        weights = [
            jnp.broadcast_to(taps[i // 3, i % 3 : i % 3 + 1, t * 128 : t * 128 + 128].astype(F32) * 0.5, (16, 128)).astype(BF)
            for i in range(9)
        ]

        def depthwise(i, sums):
            y = i * DEPTH_ROWS
            accs = [None] * DEPTH_ROWS
            for r in range(DEPTH_ROWS + 2):
                cells = hid[t, y + r]
                for q in range(max(0, r - 2), min(DEPTH_ROWS, r + 1)):
                    for s in range(3):
                        term = weights[(r - q) * 3 + s][None] * cells[s : s + 8]
                        accs[q] = term if accs[q] is None else accs[q] + term
                if r >= 2:
                    a = twice_gelu(accs[r - 2])
                    act[t, y + r - 2] = a
                    b = a[:4] + a[4:]
                    b = b[:2] + b[2:]
                    sums = sums + (b[0] + b[1]).astype(F32)
            return sums

        sums = lax.fori_loop(0, 32 // DEPTH_ROWS, depthwise, jnp.zeros((16, 128), F32))
        total[t : t + 1, :] = jnp.sum(sums, axis=0, keepdims=True)

    ar1[me] = total[...]
    exchange(lambda device, share: total, ar1.at[me], ar_send.at[0], ar_recv.at[0], ORDER)
    for load in loads[5:]:
        load.wait()
    for s in range(2):
        w_vt[s] = w_in[s, :, 512:].astype(F32).T.astype(BF)
    bias_tables(offsets, flat, bias)
    rest = ar1.at[pl.ds(0, 63)]
    pltpu.make_async_copy(rest, rest, ar_recv.at[0]).wait()
    ar2[core] = jnp.sum(ar1[...], axis=0)
    sibling = pltpu.make_async_remote_copy(
        src_ref=ar2.at[core], dst_ref=ar2.at[core], send_sem=ar_send.at[1], recv_sem=ar_recv.at[1],
        device_id=(g * 2 + 1 - core, col), device_id_type=MESH)
    sibling.start()
    sibling.wait()
    mean = jnp.sum(ar2[...], axis=0) * (0.5 / (512 * 1024))
    squeeze = jnp.concatenate([mean[i : i + 1, :] for i in range(8)], axis=1)
    squeeze = jnp.broadcast_to(squeeze, (8, 1024))
    gate = lax.dot_general(
        squeeze, down_t[...].astype(F32), NT, precision=lax.Precision.HIGHEST, preferred_element_type=F32)
    gate = gate * jax.nn.sigmoid(gate)
    excite = jax.nn.sigmoid(
        jnp.dot(gate, up[...].astype(F32), precision=lax.Precision.HIGHEST, preferred_element_type=F32))
    excite = excite.T[:, 0:1] * 0.5
    gated[...] = (w_project[...].astype(F32) * excite).astype(BF)

    weights = (gains, w_in, w_vt, w_o, w_up, w_down, bias)

    def forward(k, c):
        cells = jnp.concatenate([act[t, pl.ds(k * 8, 8)].reshape(1024, 128) for t in range(8)], axis=1)
        for r in range(0, 1024, 256):
            put(conv, pl.ds(r, 256), dot(cells[r : r + 256], gated[...]))
        windows = []
        for m in range(8):
            short = latent[pl.ds(k * 8, 8), m * 16 : m * 16 + 16, :].astype(F32)
            for j in range(2):
                branch = take(conv, 2 * m + j, 64, 16)
                windows.append((branch + short[:, j * 8 : j * 8 + 8].reshape(64, 256)).astype(BF).astype(F32))
        done = section_rows(jnp.concatenate(windows, axis=0), 0, *weights)
        for u in range(8):
            line = jnp.concatenate([done[n * 64 + u * 8 : n * 64 + u * 8 + 8] for n in range(16)], axis=0)
            fwd_send[k, u * 8 : u * 8 + 8] = line.astype(BF).reshape(8, 16, 256)
        pltpu.make_async_copy(fwd_send.at[k, me], fwd_recv.at[k, me], fr_sems.at[k]).start()

        exchange(lambda device, share: fwd_send.at[k, device], fwd_recv.at[k, me], fs_sems.at[k], fr_sems.at[k], ORDER)
        return c

    lax.fori_loop(0, BANDS, forward, 0)

    def backward(k, c):
        pltpu.make_async_copy(fwd_recv.at[k], fwd_recv.at[k], fr_sems.at[k]).wait()
        put(conv, pl.ds(0, 1024), fwd_recv[k].reshape(1024, 256).astype(F32))
        windows = jnp.concatenate([take(conv, n, 64, 16) for n in range(16)], axis=0)
        put(conv, pl.ds(0, 1024), section_rows(windows, 1, *weights))
        for t in range(64):
            back_send[k, t] = take(conv, t, 16, 64).astype(BF)
        here = out.at[k * 16 + g * 2 + col // 4, pl.ds(pl.multiple_of(lax.rem(col, 4) * 16, 16), 16)]
        pltpu.make_async_copy(back_send.at[k, me], here, br_sems.at[k]).start()

        exchange(lambda device, share: back_send.at[k, device], here, bs_sems.at[k], br_sems.at[k], ORDER)
        return c

    lax.fori_loop(0, BANDS, backward, 0)

    def finish(k, c):
        band = out.at[pl.ds(k * 16, 16)]
        pltpu.make_async_copy(band, band, br_sems.at[k]).wait()
        for sems, buf in ((fs_sems, fwd_send), (bs_sems, back_send)):
            sent = buf.at[k, pl.ds(0, 63)]
            pltpu.make_async_copy(sent, sent, sems.at[k]).wait()
        return c

    lax.fori_loop(0, BANDS, finish, 0)
    pltpu.make_async_copy(rest, rest, ar_send.at[0]).wait()


EXPAND_ROWS = 8
DEPTH_ROWS = 4


def hops(offset):
    return sum(min(d, 4 - d) for d in offset)


ORDER = sorted(
    ((dx, dy, dz) for dx in range(4) for dy in range(4) for dz in range(4) if (dx, dy, dz) != (0, 0, 0)),
    key=lambda o: (-hops(o), min(o, tuple(-d % 4 for d in o))[::-1]),
)


def per_device(
    latent, w_expand, w_depth, squeeze_down, squeeze_up, w_project,
    norm_gain, attend_in, attend_out, offset_bias, mixer_up, mixer_down,
):
    hbm = pl.BlockSpec(memory_space=pl.ANY)
    block = (BANDS, 64, 16, 256)
    dma = pltpu.SemaphoreType.DMA
    return pl.pallas_call(
        kernel,
        out_shape=jax.ShapeDtypeStruct((64, 64, 256), BF),
        in_specs=[hbm] * 12,
        out_specs=hbm,
        scratch_shapes=[
            pltpu.VMEM((32, 16, 256), BF),
            pltpu.VMEM((32, 16, 256), BF),
            pltpu.VMEM((32, 128, 256), BF),
            pltpu.VMEM((256, 1024), BF),
            pltpu.VMEM((3, 3, 1024), BF),
            pltpu.VMEM((64, 1024), BF),
            pltpu.VMEM((64, 1024), BF),
            pltpu.VMEM((1024, 256), BF),
            pltpu.VMEM((2, 2, 256), F32),
            pltpu.VMEM((2, 256, 768), BF),
            pltpu.VMEM((2, 256, 256), BF),
            pltpu.VMEM((2, 15, 8, 15), F32),
            pltpu.VMEM((2, 256, 1024), BF),
            pltpu.VMEM((2, 1024, 256), BF),
            pltpu.VMEM((2, 256, 256), BF),
            pltpu.VMEM((2, 2, 256, 128), F32),
            pltpu.VMEM((1024, 256), BF),
            pltpu.VMEM((2, 4096, 128), F32),
            pltpu.VMEM((2, 32, 8, 16, 128), BF),
            pltpu.VMEM((32, 256), BF),
            pltpu.VMEM((32, 256), BF),
            pltpu.VMEM((32, 256), BF),
            pltpu.VMEM((32, 256), BF),
            pltpu.VMEM((128, 256), BF),
            pltpu.VMEM((128, 256), BF),
            pltpu.VMEM((4, 16, 256), BF),
            pltpu.VMEM((8, 34, 10, 16, 128), BF),
            pltpu.VMEM((8, 128, 128), F32),
            pltpu.VMEM((8, 32, 8, 16, 128), BF),
            pltpu.VMEM((8, 128), F32),
            pltpu.VMEM((64, 8, 128), F32),
            pltpu.VMEM((2, 8, 128), F32),
            pltpu.VMEM((2, 1024, 128), F32),
            pltpu.VMEM(block, BF),
            pltpu.VMEM(block, BF),
            pltpu.VMEM(block, BF),
            dma((14,)),
            dma((8,)),
            dma((8,)),
            dma((2,)),
            dma((2,)),
            dma((BANDS,)),
            dma((BANDS,)),
            dma((BANDS,)),
            dma((BANDS,)),
        ],
        compiler_params=pltpu.CompilerParams(collective_id=0, has_side_effects=True, vmem_limit_bytes=46 << 20),
        name="block",
    )(*(pltpu.with_memory_space_constraint(a, pltpu.HBM) for a in (
        latent, w_expand, w_depth, squeeze_down.T, squeeze_up, w_project,
        norm_gain, attend_in, attend_out, offset_bias.transpose(0, 2, 1, 3), mixer_up, mixer_down,
    ))).reshape(32, 128, 256)


def solution(mesh):
    in_specs = (P("row", "col", None),) + (P(),) * 11
    return jax.shard_map(
        per_device, mesh=mesh, in_specs=in_specs, out_specs=P("row", "col", None), check_vma=False
    )
```

```python
import math

import jax
import jax.numpy as jnp
from jax import lax
from jax.experimental import pallas as pl
from jax.experimental.pallas import tpu as pltpu
from jax.sharding import PartitionSpec as P

MESH = pl.DeviceIdType.MESH
BF = jnp.bfloat16
F32 = jnp.float32
EPSILON = 1e-05
LOG2E = 1.4426950408889634
ROWS, COLS = 16, 8
BANDS = 4
NT = (((1,), (1,)), ((), ()))


def dot(a, b):
    return jnp.dot(a, b, preferred_element_type=F32)


def dot_nt(a, b):
    return lax.dot_general(a, b, NT, preferred_element_type=F32)


def twice_gelu(v):
    c1 = jnp.asarray(0.7978845608, v.dtype)
    c2 = jnp.asarray(0.7978845608 * 0.044715, v.dtype)
    return v + v * jnp.tanh(v * (c1 + c2 * (v * v)))


def normalise(x, gain):
    mean = jnp.sum(x, axis=-1, keepdims=True) * (1.0 / 256)
    centre = x - mean
    var = jnp.sum(centre * centre, axis=-1, keepdims=True) * (1.0 / 256)
    return (centre * lax.rsqrt(var + EPSILON) * gain).astype(BF)


def put(ref, rows, value):
    ref[0, rows, :] = value[:, :128]
    ref[1, rows, :] = value[:, 128:]


def take(ref, start, count, stride):
    rows = pl.ds(start, count, stride=stride)
    return jnp.concatenate([ref[0, rows, :], ref[1, rows, :]], axis=1)


def lanes(value, t):
    return value[:, t * 128 : t * 128 + 128]


def attention_pair(q2, k2, vt2, bias, s):
    lane = lax.broadcasted_iota(jnp.int32, (64, 256), 1)
    lane_head = lax.rem(lane, 128) // 32
    first = lax.broadcasted_iota(jnp.int32, (32, 128), 1) < 64
    first_out = lax.broadcasted_iota(jnp.int32, (128, 128), 1) < 64
    zero = jnp.zeros((), BF)
    z = jnp.zeros((64, 128), BF)
    z32 = jnp.zeros((32, 128), BF)
    scale = LOG2E / math.sqrt(32)
    out = []
    for half in range(2):
        f = slice(half * 128, half * 128 + 128)
        qh, kh, vh = q2[:, f], k2[:, f], vt2[f, :]
        q_block = jnp.concatenate(
            [jnp.concatenate([qh[:64], z], axis=1), jnp.concatenate([z, qh[64:]], axis=1)], axis=0)
        k_both = jnp.concatenate([kh[:64], kh[64:]], axis=1)
        k_block = jnp.concatenate([jnp.where(lane_head == h, k_both, zero) for h in range(4)], axis=0)
        scores = dot_nt(k_block, q_block) * scale + bias[s, half]
        scores = scores.reshape(4, 64, 128)
        raised = jnp.exp2(scores - jnp.max(scores, axis=1, keepdims=True))
        inverse = 1.0 / jnp.sum(raised, axis=1, keepdims=True)
        weights = raised.astype(BF).reshape(256, 128)
        swapped = jnp.concatenate([vh[:, 64:], vh[:, :64]], axis=1)
        lhs = []
        for w in range(2):
            for h in range(4):
                source = (vh if h % 2 == w else swapped)[h * 32 : h * 32 + 32]
                kept = jnp.where(first, source, zero) if h % 2 == 0 else jnp.where(first, zero, source)
                lhs.append(jnp.concatenate([kept, z32] if h < 2 else [z32, kept], axis=1))
        mixed = dot(jnp.concatenate(lhs, axis=0), weights)
        mixed = jnp.where(first_out, mixed[:128], mixed[128:]).reshape(4, 32, 128) * inverse
        out.append(mixed.reshape(128, 128))
    return jnp.concatenate(out, axis=0)


def section_rows(x, s, gains, w_in, w_vt, w_o, w_up, w_down, bias):
    n = x.shape[0]
    normed = normalise(x, gains[s, 0:1])
    qk = dot(normed, w_in[s, :, :512]).astype(BF)
    vt = dot_nt(w_vt[s], normed).astype(BF)
    mixes = []
    for p in range(n // 128):
        r = slice(p * 128, p * 128 + 128)
        mixed = attention_pair(qk[r, :256], qk[r, 256:], vt[:, r], bias, s)
        mixes.append(mixed.T.astype(BF))
    closed = []
    for i in range(0, n // 128, 4):
        mix = jnp.concatenate(mixes[i : i + 4], axis=0)
        closed.append((x[i * 128 : i * 128 + 512] + dot(mix, w_o[s])).astype(BF).astype(F32))
    normed = jnp.concatenate([normalise(a, gains[s, 1:2]) for a in closed], axis=0)
    attended = jnp.concatenate(closed, axis=0)
    low = []
    for r in range(n // 256):
        rows = normed[r * 256 : r * 256 + 256]
        up = [twice_gelu(dot(rows, w_up[s, :, t * 256 : t * 256 + 256]).astype(BF)) for t in range(4)]
        low.append(dot(jnp.concatenate(up, axis=1), w_down[s]))
    return attended + 0.5 * jnp.concatenate(low, axis=0)


def bias_tables(offsets, flat, bias):
    pad = jnp.zeros((8, 113), F32)
    parts = []
    for s in range(2):
        for tile in range(2):
            acc = jnp.zeros((8, 128), F32)
            for r in range(tile * 8, min(tile * 8 + 8, 15)):
                row = jnp.concatenate([offsets[s, r] * LOG2E, pad], axis=1)
                shift = (r - tile * 8) * 16
                acc = acc + (pltpu.roll(row, shift, 1) if shift else row)
            parts.append(acc)
    table = jnp.concatenate(
        [jnp.concatenate(parts[:2], axis=1), jnp.concatenate(parts[2:], axis=1)], axis=0)
    high = table.astype(BF)
    rest = table - high.astype(F32)
    middle = rest.astype(BF)
    low = (rest - middle.astype(F32)).astype(BF)
    source = lax.broadcasted_iota(jnp.int32, (256, 128), 0)
    target = lax.broadcasted_iota(jnp.int32, (256, 128), 1)
    same_row = source // 16 == target // 8
    for key_col in range(8):
        pick = same_row & (lax.rem(source, 16) == lax.rem(target, 8) + (7 - key_col))
        pick = jnp.where(pick, 1.0, 0.0).astype(BF)
        flat[0, key_col * 16 : key_col * 16 + 16, :] = dot(high, pick) + dot(middle, pick) + dot(low, pick)
    left = lax.broadcasted_iota(jnp.int32, (8, 128), 1) < 64
    for s in range(2):
        for h in range(8):
            block = flat[0, pl.ds(s * 8 + h, 8, stride=16), :]
            for key_row in range(8):
                first = pltpu.roll(block, (128 - (7 - key_row) * 8) % 128, 1) if key_row < 7 else block
                both = jnp.where(left, first, pltpu.roll(first, 64, 1))
                start = (h % 4) * 64 + key_row * 8
                bias[s, h // 4, start : start + 8, :] = both


def kernel(
    latent_hbm, w_expand_hbm, taps_hbm, down_hbm, up_hbm, w_project_hbm, gains_hbm, w_in_hbm, w_o_hbm, offsets_hbm,
    w_up_hbm, w_down_hbm,
    out,
    side_l, side_r, latent, w_expand, taps, down_t, up, w_project, gains, w_in, w_o, offsets, w_up, w_down,
    w_vt, bias, gated,
    flat, lat, edge_l, edge_r, halo_l, halo_r, halo_t, halo_b, corners, hid, hid_edge, act,
    total, ar1, ar2, conv, fwd_send, fwd_recv, back_send,
    load_sems, send_sems, recv_sems, ar_send, ar_recv, fs_sems, fr_sems, bs_sems, br_sems,
):
    row, col = lax.axis_index("row"), lax.axis_index("col")
    core, g = lax.rem(row, 2), row // 2
    me = g * 8 + col
    up_row, dn_row = lax.rem(row + ROWS - 1, ROWS), lax.rem(row + 1, ROWS)
    lf, rt = lax.rem(col + COLS - 1, COLS), lax.rem(col + 1, COLS)
    z, ylo, yhi, x = g // 2, lax.rem(g, 2), col // 4, lax.rem(col, 4)
    y = yhi * 2 + ylo

    xs = [lax.rem(x + d, 4) for d in range(4)]
    ys = [lax.rem(y + d, 4) for d in range(4)]
    zs = [lax.rem(z + d, 4) for d in range(4)]
    groups = [[zs[dz] * 2 + lax.rem(ys[dy], 2) for dy in range(4)] for dz in range(4)]
    columns = [[(ys[dy] // 2) * 4 + xs[dx] for dx in range(4)] for dy in range(4)]

    parity = lax.rem(x + y + z, 2)
    depths = [zs[dz] * 16 for dz in range(4)]
    heights = [(ys[dy] // 2) * 8 + lax.rem(ys[dy], 2) * 2 for dy in range(4)]
    halves = [xs[dx] // 2 for dx in range(4)]
    own = z * 16 + (y // 2) * 8 + parity * 4 + lax.rem(y, 2) * 2 + x // 2

    def exchange(source, target, send_sem, recv_sem, offsets):
        for dx, dy, dz in offsets:
            group, column = groups[dz][dy], columns[dy][dx]
            pltpu.make_async_remote_copy(
                src_ref=source(group * 8 + column, depths[dz] + heights[dy] + halves[dx]), dst_ref=target,
                send_sem=send_sem, recv_sem=recv_sem, device_id=(group * 2 + core, column), device_id_type=MESH).start()

    pairs = (
        (latent_hbm.at[:, pl.ds(0, 16), :], side_l), (latent_hbm.at[:, pl.ds(112, 16), :], side_r),
        (latent_hbm, latent), (w_expand_hbm, w_expand), (taps_hbm, taps), (down_hbm, down_t), (up_hbm, up),
        (w_project_hbm, w_project), (gains_hbm, gains), (w_in_hbm, w_in), (w_o_hbm, w_o), (offsets_hbm, offsets),
        (w_up_hbm, w_up), (w_down_hbm, w_down),
    )
    loads = [pltpu.make_async_copy(src, dst, load_sems.at[i]) for i, (src, dst) in enumerate(pairs)]
    for load in loads:
        load.start()

    barrier = pltpu.get_barrier_semaphore()
    for who in ((row, lf), (row, rt), (up_row, col), (dn_row, col), (up_row, lf), (up_row, rt), (dn_row, lf), (dn_row, rt)):
        pl.semaphore_signal(barrier, inc=1, device_id=who, device_id_type=MESH)

    for dx, dy, dz in ORDER:
        pl.semaphore_signal(barrier, inc=1, device_id=(groups[dz][dy] * 2 + core, columns[dy][dx]), device_id_type=MESH)
    loads[0].wait()
    loads[1].wait()

    edge_l[...] = side_l[...].astype(F32)[:, 0, :].astype(BF)
    edge_r[...] = side_r[...].astype(F32)[:, 15, :].astype(BF)
    pl.semaphore_wait(barrier, 8 + 63)
    first, last = pl.ds(0, 16), pl.ds(16, 16)
    moves = (
        (edge_l, halo_r, (row, lf)),
        (edge_r, halo_l, (row, rt)),
        (latent_hbm.at[0], halo_b, (up_row, col)),
        (latent_hbm.at[31], halo_t, (dn_row, col)),
        (edge_l.at[first], corners.at[3], (up_row, lf)),
        (edge_r.at[first], corners.at[2], (up_row, rt)),
        (edge_l.at[last], corners.at[1], (dn_row, lf)),
        (edge_r.at[last], corners.at[0], (dn_row, rt)),
    )
    copies = []
    for i, (src, dst, who) in enumerate(moves):
        copy = pltpu.make_async_remote_copy(
            src_ref=src, dst_ref=dst, send_sem=send_sems.at[i], recv_sem=recv_sems.at[i], device_id=who, device_id_type=MESH
        )
        copy.start()
        copies.append(copy)

    loads[2].wait()

    def spread(y, c):
        put(flat, pl.ds(pl.multiple_of(y * 128, 128), 128), latent[y].astype(F32))
        for v in range(8):
            for j in range(2):
                lat[j, y, v] = flat[j, pl.ds(y * 128 + v, 16, stride=8), :].astype(BF)
        return c

    lax.fori_loop(0, 32, spread, 0)
    def expand(i, c):
        rows = pl.ds(i * EXPAND_ROWS, EXPAND_ROWS)
        n = EXPAND_ROWS * 128
        cells = jnp.concatenate([lat[0, rows].reshape(n, 128), lat[1, rows].reshape(n, 128)], axis=1)
        for t in range(4):
            h = twice_gelu(dot(cells, w_expand[:, t * 256 : t * 256 + 256]).astype(BF))
            for j in range(2):
                hid[2 * t + j, pl.ds(1 + i * EXPAND_ROWS, EXPAND_ROWS), 1:9] = lanes(h, j).reshape(EXPAND_ROWS, 8, 16, 128)
        return c

    loads[3].wait()
    lax.fori_loop(0, 32 // EXPAND_ROWS, expand, 0)
    for copy in copies:
        copy.wait_recv()
    zero = jnp.zeros((), BF)
    edge_rows = []
    for i, (halo, inside) in enumerate(((halo_t, row > 0), (halo_b, row < ROWS - 1))):
        put(flat, pl.ds(i * 128, 128), halo[...].astype(F32))
        cells = jnp.concatenate([take(flat, i * 128 + v, 16, 8) for v in range(8)], axis=0)
        edge_rows.append(jnp.where(inside, cells, 0.0).astype(BF))
    left = jnp.concatenate([
        halo_l[...], jnp.where(row > 0, corners[0], zero), jnp.where(row < ROWS - 1, corners[2], zero)], axis=0)
    right = jnp.concatenate([
        halo_r[...], jnp.where(row > 0, corners[1], zero), jnp.where(row < ROWS - 1, corners[3], zero)], axis=0)
    left = jnp.where(col > 0, left, zero)
    right = jnp.where(col < COLS - 1, right, zero)
    around = jnp.concatenate(edge_rows + [left, right], axis=0)
    for t in range(4):
        h = twice_gelu(dot(around, w_expand[:, t * 256 : t * 256 + 256]).astype(BF))
        for j in range(2):
            part = lanes(h, j)
            hid[2 * t + j, 0, 1:9] = part[:128].reshape(8, 16, 128)
            hid[2 * t + j, 33, 1:9] = part[128:256].reshape(8, 16, 128)
            hid_edge[2 * t + j] = part[256:].astype(F32)

    loads[4].wait()
    place_n = lax.broadcasted_iota(jnp.int32, (16, 128), 0)

    def wrap(i, c):
        for y in (2 * i, 2 * i + 1):
            place = jnp.where(y == 0, 47, jnp.where(y == 33, 48, y - 1))
            for t in range(8):
                before = pltpu.roll(hid[t, y, 8].astype(F32), 1, 0)
                hid[t, y, 0] = jnp.where(place_n == 0, hid_edge[t, pl.ds(place, 1), :], before).astype(BF)
                after = pltpu.roll(hid[t, y, 1].astype(F32), 15, 0)
                hid[t, y, 9] = jnp.where(place_n == 15, hid_edge[t, pl.ds(place + 64, 1), :], after).astype(BF)
        return c

    lax.fori_loop(0, 17, wrap, 0)

    for t in range(8):
        weights = [
            jnp.broadcast_to(taps[i // 3, i % 3 : i % 3 + 1, t * 128 : t * 128 + 128].astype(F32) * 0.5, (16, 128)).astype(BF)
            for i in range(9)
        ]

        def depthwise(i, sums):
            y = i * DEPTH_ROWS
            accs = [None] * DEPTH_ROWS
            for r in range(DEPTH_ROWS + 2):
                cells = hid[t, y + r]
                for q in range(max(0, r - 2), min(DEPTH_ROWS, r + 1)):
                    for s in range(3):
                        term = weights[(r - q) * 3 + s][None] * cells[s : s + 8]
                        accs[q] = term if accs[q] is None else accs[q] + term
                if r >= 2:
                    a = twice_gelu(accs[r - 2])
                    act[t, y + r - 2] = a
                    b = a[:4] + a[4:]
                    b = b[:2] + b[2:]
                    sums = sums + (b[0] + b[1]).astype(F32)
            return sums

        sums = lax.fori_loop(0, 32 // DEPTH_ROWS, depthwise, jnp.zeros((16, 128), F32))
        total[t : t + 1, :] = jnp.sum(sums, axis=0, keepdims=True)

    ar1[me] = total[...]
    exchange(lambda device, share: total, ar1.at[me], ar_send.at[0], ar_recv.at[0], ORDER)
    for load in loads[5:]:
        load.wait()
    for s in range(2):
        w_vt[s] = w_in[s, :, 512:].astype(F32).T.astype(BF)
    bias_tables(offsets, flat, bias)
    rest = ar1.at[pl.ds(0, 63)]
    pltpu.make_async_copy(rest, rest, ar_recv.at[0]).wait()
    ar2[core] = jnp.sum(ar1[...], axis=0)
    sibling = pltpu.make_async_remote_copy(
        src_ref=ar2.at[core], dst_ref=ar2.at[core], send_sem=ar_send.at[1], recv_sem=ar_recv.at[1],
        device_id=(g * 2 + 1 - core, col), device_id_type=MESH)
    sibling.start()
    sibling.wait_recv()
    mean = jnp.sum(ar2[...], axis=0) * (0.5 / (512 * 1024))
    squeeze = jnp.concatenate([mean[i : i + 1, :] for i in range(8)], axis=1)
    squeeze = jnp.broadcast_to(squeeze, (8, 1024))
    gate = lax.dot_general(
        squeeze, down_t[...].astype(F32), NT, precision=lax.Precision.HIGHEST, preferred_element_type=F32)
    gate = gate * jax.nn.sigmoid(gate)
    excite = jax.nn.sigmoid(
        jnp.dot(gate, up[...].astype(F32), precision=lax.Precision.HIGHEST, preferred_element_type=F32))
    excite = excite.T[:, 0:1] * 0.5
    gated[...] = (w_project[...].astype(F32) * excite).astype(BF)

    weights = (gains, w_in, w_vt, w_o, w_up, w_down, bias)

    def forward(k, c):
        cells = jnp.concatenate([act[t, pl.ds(k * 8, 8)].reshape(1024, 128) for t in range(8)], axis=1)
        for r in range(0, 1024, 256):
            put(conv, pl.ds(r, 256), dot(cells[r : r + 256], gated[...]))
        windows = []
        for m in range(8):
            short = latent[pl.ds(k * 8, 8), m * 16 : m * 16 + 16, :].astype(F32)
            for j in range(2):
                branch = take(conv, 2 * m + j, 64, 16)
                windows.append((branch + short[:, j * 8 : j * 8 + 8].reshape(64, 256)).astype(BF).astype(F32))
        done = section_rows(jnp.concatenate(windows, axis=0), 0, *weights)
        for u in range(8):
            line = jnp.concatenate([done[n * 64 + u * 8 : n * 64 + u * 8 + 8] for n in range(16)], axis=0)
            fwd_send[k, u * 8 : u * 8 + 8] = line.astype(BF).reshape(8, 16, 256)
        pltpu.make_async_copy(fwd_send.at[k, me], fwd_recv.at[k, me], fr_sems.at[k]).start()

        exchange(lambda device, share: fwd_send.at[k, device], fwd_recv.at[k, me], fs_sems.at[k], fr_sems.at[k], ORDER)
        return c

    lax.fori_loop(0, BANDS, forward, 0)

    def backward(k, c):
        pltpu.make_async_copy(fwd_recv.at[k], fwd_recv.at[k], fr_sems.at[k]).wait()
        put(conv, pl.ds(0, 1024), fwd_recv[k].reshape(1024, 256).astype(F32))
        windows = jnp.concatenate([take(conv, n, 64, 16) for n in range(16)], axis=0)
        put(conv, pl.ds(0, 1024), section_rows(windows, 1, *weights))
        for t in range(64):
            back_send[k, t] = take(conv, t, 16, 64).astype(BF)
        here = out.at[k * 16 + g * 2 + col // 4, pl.ds(pl.multiple_of(lax.rem(col, 4) * 16, 16), 16)]
        pltpu.make_async_copy(back_send.at[k, me], here, br_sems.at[k]).start()

        exchange(lambda device, share: back_send.at[k, device], here, bs_sems.at[k], br_sems.at[k], ORDER)
        return c

    lax.fori_loop(0, BANDS, backward, 0)

    def finish(k, c):
        band = out.at[pl.ds(k * 16, 16)]
        pltpu.make_async_copy(band, band, br_sems.at[k]).wait()
        for sems, buf in ((fs_sems, fwd_send), (bs_sems, back_send)):
            sent = buf.at[k, pl.ds(0, 63)]
            pltpu.make_async_copy(sent, sent, sems.at[k]).wait()
        return c

    lax.fori_loop(0, BANDS, finish, 0)
    pltpu.make_async_copy(rest, rest, ar_send.at[0]).wait()
    for copy in copies + [sibling]:
        copy.wait_send()


EXPAND_ROWS = 8
DEPTH_ROWS = 8


def hops(offset):
    return sum(min(d, 4 - d) for d in offset)


ORDER = sorted(
    ((dx, dy, dz) for dx in range(4) for dy in range(4) for dz in range(4) if (dx, dy, dz) != (0, 0, 0)),
    key=lambda o: (-hops(o), min(o, tuple(-d % 4 for d in o))[::-1]),
)


def per_device(
    latent, w_expand, w_depth, squeeze_down, squeeze_up, w_project,
    norm_gain, attend_in, attend_out, offset_bias, mixer_up, mixer_down,
):
    hbm = pl.BlockSpec(memory_space=pl.ANY)
    block = (BANDS, 64, 16, 256)
    dma = pltpu.SemaphoreType.DMA
    return pl.pallas_call(
        kernel,
        out_shape=jax.ShapeDtypeStruct((64, 64, 256), BF),
        in_specs=[hbm] * 12,
        out_specs=hbm,
        scratch_shapes=[
            pltpu.VMEM((32, 16, 256), BF),
            pltpu.VMEM((32, 16, 256), BF),
            pltpu.VMEM((32, 128, 256), BF),
            pltpu.VMEM((256, 1024), BF),
            pltpu.VMEM((3, 3, 1024), BF),
            pltpu.VMEM((64, 1024), BF),
            pltpu.VMEM((64, 1024), BF),
            pltpu.VMEM((1024, 256), BF),
            pltpu.VMEM((2, 2, 256), F32),
            pltpu.VMEM((2, 256, 768), BF),
            pltpu.VMEM((2, 256, 256), BF),
            pltpu.VMEM((2, 15, 8, 15), F32),
            pltpu.VMEM((2, 256, 1024), BF),
            pltpu.VMEM((2, 1024, 256), BF),
            pltpu.VMEM((2, 256, 256), BF),
            pltpu.VMEM((2, 2, 256, 128), F32),
            pltpu.VMEM((1024, 256), BF),
            pltpu.VMEM((2, 4096, 128), F32),
            pltpu.VMEM((2, 32, 8, 16, 128), BF),
            pltpu.VMEM((32, 256), BF),
            pltpu.VMEM((32, 256), BF),
            pltpu.VMEM((32, 256), BF),
            pltpu.VMEM((32, 256), BF),
            pltpu.VMEM((128, 256), BF),
            pltpu.VMEM((128, 256), BF),
            pltpu.VMEM((4, 16, 256), BF),
            pltpu.VMEM((8, 34, 10, 16, 128), BF),
            pltpu.VMEM((8, 128, 128), F32),
            pltpu.VMEM((8, 32, 8, 16, 128), BF),
            pltpu.VMEM((8, 128), F32),
            pltpu.VMEM((64, 8, 128), F32),
            pltpu.VMEM((2, 8, 128), F32),
            pltpu.VMEM((2, 1024, 128), F32),
            pltpu.VMEM(block, BF),
            pltpu.VMEM(block, BF),
            pltpu.VMEM(block, BF),
            dma((14,)),
            dma((8,)),
            dma((8,)),
            dma((2,)),
            dma((2,)),
            dma((BANDS,)),
            dma((BANDS,)),
            dma((BANDS,)),
            dma((BANDS,)),
        ],
        compiler_params=pltpu.CompilerParams(collective_id=0, has_side_effects=True, vmem_limit_bytes=46 << 20),
        name="block",
    )(*(pltpu.with_memory_space_constraint(a, pltpu.HBM) for a in (
        latent, w_expand, w_depth, squeeze_down.T, squeeze_up, w_project,
        norm_gain, attend_in, attend_out, offset_bias.transpose(0, 2, 1, 3), mixer_up, mixer_down,
    ))).reshape(32, 128, 256)


def solution(mesh):
    in_specs = (P("row", "col", None),) + (P(),) * 11
    return jax.shard_map(
        per_device, mesh=mesh, in_specs=in_specs, out_specs=P("row", "col", None), check_vma=False
    )
```
